512 devices in a mesh: dp: 64 (over z, x), tensor: 8 (over y, core).
Axes of the slice: x: 4, y: 4, z: 16, core: 2. Of those that a mesh axis runs over, the one named last changes fastest.
Arguments:
- grads: float32 [64, 8, 524288], P('dp', 'tensor'), may hold values from -16 to 16
- piece_lengths: int32 [40], replicated, may hold values from 1 to 65536
- split_flags: int32 [40], replicated, may hold values from 0 to 1
- master_params: float32 [8, 524288], P('tensor', 'dp'), may hold values from -16 to 16
- exp_avg: float32 [8, 524288], P('tensor', 'dp'), may hold values from -0.3 to 0.3
- exp_avg_sq: float32 [8, 524288], P('tensor', 'dp'), may hold values from 0.001 to 0.1
Outputs:
- new_master: float32 [8, 524288], P('tensor', 'dp')
- new_avg: float32 [8, 524288], P('tensor', 'dp')
- new_avg_sq: float32 [8, 524288], P('tensor', 'dp')
- model_params: bfloat16 [8, 524288], P('tensor')
The draws below stay inside these ranges and needn't reach their ends.
All inputs are finite; a program needn't handle non-finite values.
Results may differ from the reference program's by a relative error of at most 0.0004.
Values may be sent and summed in bfloat16 or wider, within the bound.
A program may use at most 64 MiB of HBM per device.

```python
import math
import jax
import jax.numpy as jnp
from jax import lax

NPIECE = 40
BUCKET = 524288
N_DP = 64
N_TENSOR = 8


def piece_layout(key):
    folded = jax.random.fold_in(key, 21)
    key_short = jax.random.fold_in(folded, 1)
    key_weight = jax.random.fold_in(folded, 2)
    key_flag = jax.random.fold_in(folded, 3)
    key_order = jax.random.fold_in(folded, 4)
    largest = BUCKET // 8
    shorts = jax.random.randint(key_short, (4,), 1, 4, dtype=jnp.int32)
    shorts = jnp.where(jnp.arange(4, dtype=jnp.int32) == 0, 1, shorts).astype(jnp.int32)
    others = NPIECE - 5
    surplus = (BUCKET - largest - others - jnp.sum(shorts)).astype(jnp.int32)
    weights = jax.random.randint(key_weight, (others,), 1, 5, dtype=jnp.int32)
    portion = surplus * weights // jnp.sum(weights)
    leftover = surplus - jnp.sum(portion)
    lengths_rest = 1 + portion + (jnp.arange(others, dtype=jnp.int32) < leftover).astype(jnp.int32)
    lengths_all = jnp.concatenate([jnp.full((1,), largest, jnp.int32), shorts, lengths_rest.astype(jnp.int32)])
    flagged = jax.random.randint(key_flag, (NPIECE,), 0, 2, dtype=jnp.int32)
    index_all = jnp.arange(NPIECE, dtype=jnp.int32)
    flagged = jnp.where((index_all >= 1) & (index_all <= 2), 0, flagged).astype(jnp.int32)
    ordering = jax.random.permutation(key_order, NPIECE)
    return (lengths_all[ordering].astype(jnp.int32), flagged[ordering].astype(jnp.int32))


def draw_piece_lengths(key, part):
    return piece_layout(key)[0]


def draw_split_flags(key, part):
    return piece_layout(key)[1]


def draw_master_params(key, part):
    first = jax.random.fold_in(key, 11)
    second = jax.random.fold_in(key, 12)
    position = jnp.arange(BUCKET, dtype=jnp.float32)[None, :]
    rising = 0.5 + 1.5 * position / BUCKET
    rough = jnp.exp(jax.random.uniform(second, (N_TENSOR, BUCKET), jnp.float32, -0.69, 0.69))
    base = jnp.clip(jax.random.normal(first, (N_TENSOR, BUCKET), jnp.float32), -4.0, 4.0)
    return (base * rising * rough).astype(jnp.float32)


def raised(array, stream_key, source, target, parts, factor):
    owner, partner = [(jnp.arange(array.shape[dim]) // (array.shape[dim] // parts)).reshape([-1 if axis == dim else 1 for axis in range(array.ndim)]) for dim in (source, target)]
    chosen = jax.random.permutation(stream_key, parts)[partner]
    strong = (owner == chosen) | (owner == (partner + parts // 2) % parts)
    return jnp.where(strong, factor * array, array)


def level_of(stream_key, extent, shards, low, high):
    def one(dim, shards_of):
        heights = jax.random.uniform(jax.random.fold_in(jax.random.fold_in(stream_key, 6), dim), (shards_of,), jnp.float32, low / len(shards), high / len(shards))
        return jnp.repeat(jnp.exp(heights), extent[dim] // shards_of).reshape((-1,) + (1,) * (len(extent) - dim - 1))

    factor_of = one(*shards[0])
    for cut in shards[1:]:
        factor_of = factor_of * one(*cut)
    return factor_of


def bell_draw(rng, extent, deviation, reach, pieces=(), held_as=jnp.bfloat16):
    array = deviation * jax.random.normal(rng, extent, jnp.float32)
    if pieces:
        array = array * level_of(rng, extent, pieces, -0.22, 0.18)
    return jnp.clip(array, -reach, reach).astype(held_as)


def gaussian_with(own_key, dims, width, reach, shards, heavy, kind=jnp.bfloat16):
    drawn = width * jax.random.normal(own_key, dims, jnp.float32)
    if shards:
        drawn = drawn * level_of(own_key, dims, shards, -0.22, 0.18)
    return jnp.clip(raised(drawn, jax.random.fold_in(own_key, 3), *heavy), -reach, reach).astype(kind)


def setup_inputs(seed: int = 0) -> dict:
    keys = jax.random.split(jax.random.key(seed), 7)
    grads = gaussian_with(keys[0], (N_DP, N_TENSOR, BUCKET), 1.0, 16.0, ((0, 64), (1, 8)), (0, 2, 64, 4.0), jnp.float32)
    piece_lengths = draw_piece_lengths(jax.random.fold_in(keys[6], 71), 0)
    split_flags = draw_split_flags(jax.random.fold_in(keys[6], 71), 0)
    master_params = draw_master_params(jax.random.fold_in(keys[6], 71), 0)
    exp_avg = bell_draw(keys[4], (N_TENSOR, BUCKET), 0.05, 0.3, ((0, 8), (1, 64)), jnp.float32)
    exp_avg_sq = jnp.clip(jnp.exp(math.log(0.1) - 4.6051702 * jax.random.uniform(keys[5], (N_TENSOR, BUCKET), jnp.float32) ** level_of(keys[5], (N_TENSOR, BUCKET), ((0, 8), (1, 64)), -0.2, 0.2)), 0.001, 0.1)
    return dict(grads=grads, piece_lengths=piece_lengths, split_flags=split_flags, master_params=master_params, exp_avg=exp_avg, exp_avg_sq=exp_avg_sq)


def reference(grads, piece_lengths, split_flags, master_params, exp_avg, exp_avg_sq):
    grad = lax.optimization_barrier(jnp.sum(grads, axis=0)) / N_DP
    new_avg = 0.9 * exp_avg + 0.1 * grad
    new_avg_sq = 0.95 * exp_avg_sq + 0.05 * grad * grad
    update = new_avg / (jnp.sqrt(new_avg_sq) + 1e-08) + 0.1 * master_params
    ends = jnp.cumsum(piece_lengths).astype(jnp.int32)
    position = jnp.arange(BUCKET, dtype=jnp.int32)
    piece_ids = lax.optimization_barrier(jnp.sum((position[:, None] >= ends[None, :]).astype(jnp.int32), axis=1)).astype(jnp.int32)
    wsq = jax.vmap(lambda row: jax.ops.segment_sum(row * row, piece_ids, num_segments=NPIECE))(master_params)
    usq = jax.vmap(lambda row: jax.ops.segment_sum(row * row, piece_ids, num_segments=NPIECE))(update)
    split = (split_flags == 1)[None, :]
    wnorm_sq = jnp.where(split, lax.optimization_barrier(jnp.sum(wsq, axis=0, keepdims=True)), wsq)
    unorm_sq = jnp.where(split, lax.optimization_barrier(jnp.sum(usq, axis=0, keepdims=True)), usq)
    trust = jnp.sqrt(wnorm_sq) / jnp.maximum(jnp.sqrt(unorm_sq), 1.0)
    trust_at = trust[:, piece_ids]
    new_master = master_params - 0.05 * trust_at * update
    model_params = new_master.astype(jnp.bfloat16)
    return (new_master, new_avg, new_avg_sq, model_params)
```

```python
import jax
import jax.numpy as jnp
from jax import lax
from jax.experimental import pallas as pl
from jax.experimental.pallas import tpu as pltpu
from jax.sharding import PartitionSpec as P

MESH = pl.DeviceIdType.MESH
NZ, NX, NT = 16, 4, 8
GROUP = 4
ROWS = 64
WORDS = 32
NP = 40
XROWS = GROUP * WORDS + 8
ORDER = (2, 1, 3, 0)


def encode(block, unit):
    top = jnp.max(jnp.abs(block), axis=0, keepdims=True)
    scale = (top * unit).astype(jnp.int32) + 1
    inverse = (32767.0 * unit) / scale.astype(jnp.float32)
    codes = jnp.round(block * inverse).astype(jnp.int32)
    return (codes[:WORDS] << 16) + codes[WORDS:], scale


def decode(words, scale, unit):
    step = scale.astype(jnp.float32) * (1.0 / (32767.0 * unit))
    high = ((words + 32768) >> 16).astype(jnp.float32) * step
    low = ((words << 16) >> 16).astype(jnp.float32) * step
    return high, low


UNIT_X = float(2**26)
UNIT_Z = float(2**24)


def piece_sums(values, position, starts):
    rows = []
    for k in range(NP):
        inside = (position >= starts[k]) & (position < starts[k + 1])
        rows.append(jnp.sum(jnp.where(inside, values, 0.0), axis=0, keepdims=True))
    table = jnp.concatenate(rows, axis=0)
    totals = jnp.sum(table, axis=1, keepdims=True)
    piece = lax.broadcasted_iota(jnp.int32, (NP, 128), 0)
    lane = lax.broadcasted_iota(jnp.int32, (NP, 128), 1)
    return jnp.sum(jnp.where(piece == lane, totals, 0.0), axis=0, keepdims=True)


def kernel(
    lengths, flags, grads, master, avg, avg_sq,
    out_master, out_avg, out_avg_sq, out_model,
    held, coded, x_in, z_out, z_in, total, state, stat_z, stat_p, weights,
    load_sem, state_sem, xs_sem, xr_sem, zs_sem, zr_sem, ns_sem, nr_sem, ps_sem, pr_sem,
    gs_sem, gr_sem, fs_sem, fr_sem,
):
    dp = lax.axis_index("dp")
    t = lax.axis_index("tensor")
    z, x = dp // NX, dp % NX
    home = z // GROUP

    def group_of(k):
        return (home + k) % GROUP

    def at(zz, xx, tt):
        return (zz * NX + xx, tt)

    def load(k):
        rows = pl.ds(pl.multiple_of(group_of(k) * 1024, 1024), 1024)
        return pltpu.make_async_copy(grads.at[rows], held.at[rows], load_sem.at[k])

    for k in ORDER:
        load(k).start()
    state_copies = [
        pltpu.make_async_copy(ref, state.at[i], state_sem.at[i])
        for i, ref in enumerate((master, avg, avg_sq))
    ]
    for copy in state_copies:
        copy.start()

    barrier = pltpu.get_barrier_semaphore()

    def hail_z(o, c):
        pl.semaphore_signal(barrier, 1, device_id=at((z + o) % NZ, x, t), device_id_type=MESH)
        return c

    lax.fori_loop(1, NZ, hail_z, 0)

    def plane(o):
        me = x * NT + t
        other = (me + o) % (NX * NT)
        return other // NT, other % NT

    def hail_p(o, c):
        xx, tt = plane(o)
        pl.semaphore_signal(barrier, 1, device_id=at(z, xx, tt), device_id_type=MESH)
        return c

    lax.fori_loop(1, NX * NT, hail_p, 0)

    def x_copy(k, o):
        a = group_of(k)
        xx = (x + o) % NX
        return pltpu.make_async_remote_copy(
            src_ref=coded.at[xx, a], dst_ref=x_in.at[x, a],
            send_sem=xs_sem.at[o, k], recv_sem=xr_sem.at[x, a],
            device_id=at(z, xx, t), device_id_type=MESH,
        )

    def x_arrival(k, o):
        a = group_of(k)
        xx = (x + o) % NX
        return pltpu.make_async_remote_copy(
            src_ref=coded.at[xx, a], dst_ref=x_in.at[xx, a],
            send_sem=xs_sem.at[o, k], recv_sem=xr_sem.at[xx, a],
            device_id=at(z, xx, t), device_id_type=MESH,
        )

    for n, k in enumerate(ORDER):
        a = group_of(k)
        load(k).wait()

        def code(o, c, a=a):
            xx = (x + o) % NX
            for j in range(GROUP):
                start = pl.multiple_of(((a * GROUP + j) * NX + xx) * ROWS, ROWS)
                words, scale = encode(held[pl.ds(start, ROWS), :], UNIT_X)
                coded[xx, a, j * WORDS : (j + 1) * WORDS, :] = words
                coded[xx, a, GROUP * WORDS + j : GROUP * WORDS + j + 1, :] = scale
            return c

        lax.fori_loop(1, NX, code, 0)
        if n == 0:
            pl.semaphore_wait(barrier, NZ - 1 + NX * NT - 1)
        for o in (2, 1, 3):
            x_copy(k, o).start()

    starts = [jnp.int32(0)]
    for k in range(NP):
        starts.append(starts[-1] + lengths[k])
    position = (
        dp * (ROWS * 128)
        + lax.broadcasted_iota(jnp.int32, (ROWS, 128), 0) * 128
        + lax.broadcasted_iota(jnp.int32, (ROWS, 128), 1)
    )
    for copy in state_copies:
        copy.wait()
    w = state[0]
    w_sums = piece_sums(w * w, position, starts)

    def z_copy(zz):
        return pltpu.make_async_remote_copy(
            src_ref=z_out.at[zz, pl.ds(0, WORDS + 1)], dst_ref=z_in.at[z, pl.ds(0, WORDS + 1)],
            send_sem=zs_sem.at[zz], recv_sem=zr_sem.at[z],
            device_id=at(zz, x, t), device_id_type=MESH,
        )

    def z_arrival(zz):
        return pltpu.make_async_remote_copy(
            src_ref=z_out.at[zz, pl.ds(0, WORDS + 1)], dst_ref=z_in.at[zz, pl.ds(0, WORDS + 1)],
            send_sem=zs_sem.at[zz], recv_sem=zr_sem.at[zz],
            device_id=at(zz, x, t), device_id_type=MESH,
        )

    def sum_over_x(a, j):
        start = pl.multiple_of(((a * GROUP + j) * NX + x) * ROWS, ROWS)
        high = held[pl.ds(start, WORDS), :]
        low = held[pl.ds(pl.multiple_of(start + WORDS, WORDS), WORDS), :]
        for o in range(1, NX):
            xx = (x + o) % NX
            rows = pl.ds(pl.multiple_of(j * WORDS, WORDS), WORDS)
            tile = x_in[xx, a, GROUP * WORDS :, :]
            picked = lax.broadcasted_iota(jnp.int32, (8, 128), 0) == j
            scale = jnp.sum(jnp.where(picked, tile, 0), axis=0, keepdims=True)
            h, l = decode(x_in[xx, a, rows, :], scale, UNIT_X)
            high, low = high + h, low + l
        return high, low

    for k in ORDER:
        a = group_of(k)
        for o in (1, 3, 2):
            x_arrival(k, o).wait_recv()

        def forward(i, c, a=a, k=k):
            j = (z + i) % GROUP
            high, low = sum_over_x(a, j)
            words, scale = encode(jnp.concatenate([high, low], axis=0), UNIT_Z)
            zz = a * GROUP + j
            z_out[zz, :WORDS, :] = words
            z_out[zz, WORDS : WORDS + 1, :] = scale
            z_copy(zz).start()
            return c

        lax.fori_loop(1 if k == 0 else 0, GROUP, forward, 0)
    high, low = sum_over_x(home, z % GROUP)
    total[:WORDS, :] = high
    total[WORDS:, :] = low

    def collect(o, c):
        zz = (z + o) % NZ
        z_arrival(zz).wait_recv()
        h, l = decode(z_in[zz, :WORDS, :], z_in[zz, WORDS : WORDS + 1, :], UNIT_Z)
        total[:WORDS, :] += h
        total[WORDS:, :] += l
        return c

    lax.fori_loop(1, NZ, collect, 0)

    grad = total[...] * (1.0 / (NZ * NX))
    new_avg = 0.9 * state[1] + 0.1 * grad
    new_avg_sq = 0.95 * state[2] + 0.05 * grad * grad
    out_avg[...] = new_avg
    out_avg_sq[...] = new_avg_sq
    update = new_avg / (jnp.sqrt(new_avg_sq) + 1e-08) + 0.1 * state[0]
    total[...] = update
    u_sums = piece_sums(update * update, position, starts)

    stat_z[z, 0:1, :] = w_sums
    stat_z[z, 1:2, :] = u_sums

    def n_copy(o):
        zz = (z + o) % NZ
        return pltpu.make_async_remote_copy(
            src_ref=stat_z.at[z, pl.ds(0, 2)], dst_ref=stat_z.at[z, pl.ds(0, 2)],
            send_sem=ns_sem.at[o], recv_sem=nr_sem.at[z],
            device_id=at(zz, x, t), device_id_type=MESH,
        )

    def n_arrival(o):
        zz = (z + o) % NZ
        return pltpu.make_async_remote_copy(
            src_ref=stat_z.at[z, pl.ds(0, 2)], dst_ref=stat_z.at[zz, pl.ds(0, 2)],
            send_sem=ns_sem.at[o], recv_sem=nr_sem.at[zz],
            device_id=at(zz, x, t), device_id_type=MESH,
        )

    for o in (8, 7, 9, 6, 10, 5, 11, 4, 12, 3, 13, 2, 14, 1, 15):
        n_copy(o).start()
    for o in range(1, NZ):
        n_arrival(o).wait_recv()
    sums = stat_z[0, 0:2, :]
    for zz in range(1, NZ):
        sums = sums + stat_z[zz, 0:2, :]
    me = x * NT + t
    stat_p[me, 0:2, :] = sums

    def p_copy(o):
        xx, tt = plane(o)
        return pltpu.make_async_remote_copy(
            src_ref=stat_p.at[me, pl.ds(0, 2)], dst_ref=stat_p.at[me, pl.ds(0, 2)],
            send_sem=ps_sem.at[o], recv_sem=pr_sem.at[me],
            device_id=at(z, xx, tt), device_id_type=MESH,
        )

    def p_arrival(o):
        xx, tt = plane(o)
        return pltpu.make_async_remote_copy(
            src_ref=stat_p.at[me, pl.ds(0, 2)], dst_ref=stat_p.at[xx * NT + tt, pl.ds(0, 2)],
            send_sem=ps_sem.at[o], recv_sem=pr_sem.at[xx * NT + tt],
            device_id=at(z, xx, tt), device_id_type=MESH,
        )

    def start_p(o, c):
        p_copy(o).start()
        return c

    def wait_p(o, c):
        p_arrival(o).wait_recv()
        return c

    lax.fori_loop(1, NX * NT, start_p, 0)
    lax.fori_loop(1, NX * NT, wait_p, 0)
    data_sum = stat_p[t, 0:2, :]
    for xx in range(1, NX):
        data_sum = data_sum + stat_p[xx * NT + t, 0:2, :]
    tensor_sum = stat_p[0, 0:2, :]
    for i in range(1, NX * NT):
        tensor_sum = tensor_sum + stat_p[i, 0:2, :]
    effective = jnp.where(flags[0:1, :] == 1, tensor_sum, data_sum)
    trust = jnp.sqrt(effective[0:1]) / jnp.maximum(jnp.sqrt(effective[1:2]), 1.0)
    trust_at = jnp.broadcast_to(trust[:, 0:1], (ROWS, 128))
    for k in range(1, NP):
        trust_at = jnp.where(position >= starts[k], trust[:, k : k + 1], trust_at)
    new_weights = state[0] - 0.05 * trust_at * total[...]
    out_master[...] = new_weights

    weights[z, x] = new_weights.astype(jnp.bfloat16)

    def g_copy(o):
        zz = (z + o) % NZ
        return pltpu.make_async_remote_copy(
            src_ref=weights.at[z, x], dst_ref=weights.at[z, x],
            send_sem=gs_sem.at[o], recv_sem=gr_sem.at[z],
            device_id=at(zz, x, t), device_id_type=MESH,
        )

    def g_arrival(zz):
        return pltpu.make_async_remote_copy(
            src_ref=weights.at[z, x], dst_ref=weights.at[zz, x],
            send_sem=gs_sem.at[1], recv_sem=gr_sem.at[zz],
            device_id=at(zz, x, t), device_id_type=MESH,
        )

    for o in (8, 7, 9, 6, 10, 5, 11, 4, 12, 3, 13, 2, 14, 1, 15):
        g_copy(o).start()

    def f_copy(k, o):
        a = group_of(k)
        xx = (x + o) % NX
        blocks = weights.at[pl.ds(a * GROUP, GROUP), x]
        return pltpu.make_async_remote_copy(
            src_ref=blocks, dst_ref=blocks,
            send_sem=fs_sem.at[o, k], recv_sem=fr_sem.at[x, a],
            device_id=at(z, xx, t), device_id_type=MESH,
        )

    def f_arrival(k, o):
        a = group_of(k)
        xx = (x + o) % NX
        blocks = weights.at[pl.ds(a * GROUP, GROUP), xx]
        return pltpu.make_async_remote_copy(
            src_ref=blocks, dst_ref=blocks,
            send_sem=fs_sem.at[o, k], recv_sem=fr_sem.at[xx, a],
            device_id=at(z, xx, t), device_id_type=MESH,
        )

    for k in (0, 1, 3, 2):
        for i in range(1 if k == 0 else 0, GROUP):
            g_arrival(group_of(k) * GROUP + (z + i) % GROUP).wait_recv()
        for o in (2, 1, 3):
            f_copy(k, o).start()
    for k in (0, 1, 3, 2):
        for o in (1, 3, 2):
            f_arrival(k, o).wait_recv()
        a = group_of(k)
        for j in range(GROUP):
            for xx in range(NX):
                start = pl.multiple_of(((a * GROUP + j) * NX + xx) * ROWS, ROWS)
                out_model[pl.ds(start, ROWS), :] = weights[a * GROUP + j, xx]

    for k in ORDER:
        for o in range(1, NX):
            x_copy(k, o).wait_send()
            f_copy(k, o).wait_send()
    for o in range(1, NZ):
        z_copy((z + o) % NZ).wait_send()
        n_copy(o).wait_send()
        g_copy(o).wait_send()

    def end_p(o, c):
        p_copy(o).wait_send()
        return c

    lax.fori_loop(1, NX * NT, end_p, 0)


def local(grads, piece_lengths, split_flags, master_params, exp_avg, exp_avg_sq):
    vmem = pl.BlockSpec(memory_space=pltpu.VMEM)
    anywhere = pl.BlockSpec(memory_space=pltpu.HBM)
    shard = jax.ShapeDtypeStruct((ROWS, 128), jnp.float32)
    dma = pltpu.SemaphoreType.DMA
    flags = jnp.pad(split_flags, (0, 128 - NP)).reshape(1, 128)
    new_master, new_avg, new_avg_sq, model = pl.pallas_call(
        kernel,
        name="lamb",
        out_shape=(shard, shard, shard, jax.ShapeDtypeStruct((NZ * NX * ROWS, 128), jnp.bfloat16)),
        in_specs=[pl.BlockSpec(memory_space=pltpu.SMEM), vmem, anywhere, anywhere, anywhere, anywhere],
        out_specs=(vmem, vmem, vmem, vmem),
        scratch_shapes=[
            pltpu.VMEM((NZ * NX * ROWS, 128), jnp.float32),
            pltpu.VMEM((NX, GROUP, XROWS, 128), jnp.int32),
            pltpu.VMEM((NX, GROUP, XROWS, 128), jnp.int32),
            pltpu.VMEM((NZ, WORDS + 8, 128), jnp.int32),
            pltpu.VMEM((NZ, WORDS + 8, 128), jnp.int32),
            pltpu.VMEM((ROWS, 128), jnp.float32),
            pltpu.VMEM((3, ROWS, 128), jnp.float32),
            pltpu.VMEM((NZ, 8, 128), jnp.float32),
            pltpu.VMEM((NX * NT, 8, 128), jnp.float32),
            pltpu.VMEM((NZ, NX, ROWS, 128), jnp.bfloat16),
            dma((4,)), dma((3,)),
            dma((NX, 4)), dma((NX, 4)),
            dma((NZ,)), dma((NZ,)),
            dma((NZ,)), dma((NZ,)),
            dma((NX * NT,)), dma((NX * NT,)),
            dma((NZ,)), dma((NZ,)),
            dma((NX, 4)), dma((NX, 4)),
        ],
        compiler_params=pltpu.CompilerParams(
            collective_id=0, has_side_effects=True, vmem_limit_bytes=24 * 2**20
        ),
    )(
        piece_lengths, flags, grads.reshape(NZ * NX * ROWS, 128), master_params.reshape(ROWS, 128),
        exp_avg.reshape(ROWS, 128), exp_avg_sq.reshape(ROWS, 128),
    )
    return (
        new_master.reshape(1, -1), new_avg.reshape(1, -1), new_avg_sq.reshape(1, -1), model.reshape(1, -1)
    )


def solution(mesh):
    return jax.shard_map(
        local,
        mesh=mesh,
        in_specs=(
            P("dp", "tensor", None),
            P(),
            P(),
            P("tensor", "dp"),
            P("tensor", "dp"),
            P("tensor", "dp"),
        ),
        out_specs=(P("tensor", "dp"), P("tensor", "dp"), P("tensor", "dp"), P("tensor", None)),
        check_vma=False,
    )
```

```python
import jax
import jax.numpy as jnp
from jax import lax
from jax.experimental import pallas as pl
from jax.experimental.pallas import tpu as pltpu
from jax.sharding import PartitionSpec as P

MESH = pl.DeviceIdType.MESH
NZ, NX, NY, NT = 16, 4, 4, 8
GROUP = 4
ROWS = 64
WORDS = 32
NP = 40
XROWS = GROUP * WORDS + 8
ORDER = (2, 1, 3, 0)


def encode(block, unit):
    top = jnp.max(jnp.abs(block), axis=0, keepdims=True)
    scale = (top * unit).astype(jnp.int32) + 1
    inverse = (32767.0 * unit) / scale.astype(jnp.float32)
    codes = jnp.round(block * inverse).astype(jnp.int32)
    return (codes[:WORDS] << 16) + codes[WORDS:], scale


def decode(words, scale, unit):
    step = scale.astype(jnp.float32) * (1.0 / (32767.0 * unit))
    high = ((words + 32768) >> 16).astype(jnp.float32) * step
    low = ((words << 16) >> 16).astype(jnp.float32) * step
    return high, low


LONG = (8, 4, 12)
SHORT = (2, 1, 15)
ARRIVALS = (1, 15, 2, 4, 12, 5, 11, 3, 13, 6, 14, 8, 7, 9, 10)

UNIT_X = float(2**26)
UNIT_Z = float(2**24)


def piece_sums(values, position, starts):
    rows = []
    for k in range(NP):
        inside = (position >= starts[k]) & (position < starts[k + 1])
        rows.append(jnp.sum(jnp.where(inside, values, 0.0), axis=0, keepdims=True))
    table = jnp.concatenate(rows, axis=0)
    totals = jnp.sum(table, axis=1, keepdims=True)
    piece = lax.broadcasted_iota(jnp.int32, (NP, 128), 0)
    lane = lax.broadcasted_iota(jnp.int32, (NP, 128), 1)
    return jnp.sum(jnp.where(piece == lane, totals, 0.0), axis=0, keepdims=True)


def kernel(
    lengths_in, flags_in, grads, master, avg, avg_sq,
    out_master, out_avg, out_avg_sq, weights,
    held, coded, x_in, z_out, z_in, total, state, made, stat_z, stat_p, lengths, flags,
    word_sem, load_sem, state_sem, out_sem, xs_sem, xr_sem, zs_sem, zr_sem, ns_sem, nr_sem, ps_sem, pr_sem,
    gs_sem, gr_sem, fs_sem, fr_sem,
):
    dp = lax.axis_index("dp")
    t = lax.axis_index("tensor")
    z, x = dp // NX, dp % NX
    home = z // GROUP

    def group_of(k):
        return (home + k) % GROUP

    def at(zz, xx, tt):
        return (zz * NX + xx, tt)

    def load(k):
        rows = pl.ds(pl.multiple_of(group_of(k) * 1024, 1024), 1024)
        return pltpu.make_async_copy(grads.at[rows], held.at[rows], load_sem.at[k])

    for k in ORDER:
        load(k).start()
    state_copies = [
        pltpu.make_async_copy(ref, state.at[i], state_sem.at[i])
        for i, ref in enumerate((master, avg, avg_sq))
    ]
    state_copies += [
        pltpu.make_async_copy(lengths_in, lengths, state_sem.at[3]),
        pltpu.make_async_copy(flags_in, flags, state_sem.at[4]),
    ]
    for copy in state_copies:
        copy.start()
    out_copies = [
        pltpu.make_async_copy(made.at[i], ref, out_sem.at[i])
        for i, ref in enumerate((out_master, out_avg, out_avg_sq))
    ]

    barrier = pltpu.get_barrier_semaphore()

    y, core = t // 2, t % 2

    def near(dx, dy, dc):
        return at(z, (x + dx) % NX, ((y + dy) % NY) * 2 + (core + dc) % 2)

    greeted = [near(dx, 0, 0) for dx in range(1, NX)]
    greeted += [near(0, dy, dc) for dy in range(NY) for dc in range(2) if dy or dc]
    greeted += [at((z + o) % NZ, x, t) for o in (1, NZ - 1)]
    for device in greeted:
        pl.semaphore_signal(barrier, 1, device_id=device, device_id_type=MESH)

    def pass_on(step):
        for o in (2**step, NZ - 2**step):
            pl.semaphore_signal(
                word_sem.at[step], 1, device_id=at((z + o) % NZ, x, t), device_id_type=MESH
            )

    def hear(step):
        pl.semaphore_wait(word_sem.at[step], 2)

    def x_copy(k, o):
        a = group_of(k)
        xx = (x + o) % NX
        return pltpu.make_async_remote_copy(
            src_ref=coded.at[xx, a], dst_ref=x_in.at[x, a],
            send_sem=xs_sem.at[o, k], recv_sem=xr_sem.at[x, a],
            device_id=at(z, xx, t), device_id_type=MESH,
        )

    def x_arrival(k, o):
        a = group_of(k)
        xx = (x + o) % NX
        return pltpu.make_async_remote_copy(
            src_ref=coded.at[xx, a], dst_ref=x_in.at[xx, a],
            send_sem=xs_sem.at[o, k], recv_sem=xr_sem.at[xx, a],
            device_id=at(z, xx, t), device_id_type=MESH,
        )

    for n, k in enumerate(ORDER):
        a = group_of(k)
        load(k).wait()

        def code(o, c, a=a):
            xx = (x + o) % NX
            for j in range(GROUP):
                start = pl.multiple_of(((a * GROUP + j) * NX + xx) * ROWS, ROWS)
                words, scale = encode(held[pl.ds(start, ROWS), :], UNIT_X)
                coded[xx, a, j * WORDS : (j + 1) * WORDS, :] = words
                coded[xx, a, GROUP * WORDS + j : GROUP * WORDS + j + 1, :] = scale
            return c

        lax.fori_loop(1, NX, code, 0)
        if n == 0:
            pl.semaphore_wait(barrier, len(greeted))
        for o in (2, 1, 3):
            x_copy(k, o).start()
        if n > 0:
            hear(n - 1)
        if n < 3:
            pass_on(n)

    for copy in state_copies:
        copy.wait()
    starts = [jnp.int32(0)]
    split = jnp.zeros((1, 128), jnp.int32)
    for k in range(NP):
        starts.append(starts[-1] + lengths[k])
        split = jnp.where(lax.broadcasted_iota(jnp.int32, (1, 128), 1) == k, flags[k], split)
    position = (
        dp * (ROWS * 128)
        + lax.broadcasted_iota(jnp.int32, (ROWS, 128), 0) * 128
        + lax.broadcasted_iota(jnp.int32, (ROWS, 128), 1)
    )
    w = state[0]
    w_sums = piece_sums(w * w, position, starts)

    def z_copy(zz):
        return pltpu.make_async_remote_copy(
            src_ref=z_out.at[zz, pl.ds(0, WORDS + 1)], dst_ref=z_in.at[z, pl.ds(0, WORDS + 1)],
            send_sem=zs_sem.at[zz], recv_sem=zr_sem.at[z],
            device_id=at(zz, x, t), device_id_type=MESH,
        )

    def z_arrival(zz):
        return pltpu.make_async_remote_copy(
            src_ref=z_out.at[zz, pl.ds(0, WORDS + 1)], dst_ref=z_in.at[zz, pl.ds(0, WORDS + 1)],
            send_sem=zs_sem.at[zz], recv_sem=zr_sem.at[zz],
            device_id=at(zz, x, t), device_id_type=MESH,
        )

    def sum_over_x(a, j):
        start = pl.multiple_of(((a * GROUP + j) * NX + x) * ROWS, ROWS)
        high = held[pl.ds(start, WORDS), :]
        low = held[pl.ds(pl.multiple_of(start + WORDS, WORDS), WORDS), :]
        for o in range(1, NX):
            xx = (x + o) % NX
            rows = pl.ds(pl.multiple_of(j * WORDS, WORDS), WORDS)
            tile = x_in[xx, a, GROUP * WORDS :, :]
            picked = lax.broadcasted_iota(jnp.int32, (8, 128), 0) == j
            scale = jnp.sum(jnp.where(picked, tile, 0), axis=0, keepdims=True)
            h, l = decode(x_in[xx, a, rows, :], scale, UNIT_X)
            high, low = high + h, low + l
        return high, low

    for k in ORDER:
        a = group_of(k)
        for o in (1, 3, 2):
            x_arrival(k, o).wait_recv()

        def forward(i, c, a=a, k=k):
            j = (z + i) % GROUP
            high, low = sum_over_x(a, j)
            words, scale = encode(jnp.concatenate([high, low], axis=0), UNIT_Z)
            zz = a * GROUP + j
            z_out[zz, :WORDS, :] = words
            z_out[zz, WORDS : WORDS + 1, :] = scale
            z_copy(zz).start()
            return c

        lax.fori_loop(1 if k == 0 else 0, GROUP, forward, 0)
    high, low = sum_over_x(home, z % GROUP)
    total[:WORDS, :] = high
    total[WORDS:, :] = low

    def collect(o, c):
        zz = (z + o) % NZ
        z_arrival(zz).wait_recv()
        h, l = decode(z_in[zz, :WORDS, :], z_in[zz, WORDS : WORDS + 1, :], UNIT_Z)
        total[:WORDS, :] += h
        total[WORDS:, :] += l
        return c

    lax.fori_loop(1, NZ, collect, 0)

    grad = total[...] * (1.0 / (NZ * NX))
    new_avg = 0.9 * state[1] + 0.1 * grad
    new_avg_sq = 0.95 * state[2] + 0.05 * grad * grad
    made[1] = new_avg
    made[2] = new_avg_sq
    out_copies[1].start()
    out_copies[2].start()
    update = new_avg / (jnp.sqrt(new_avg_sq) + 1e-08) + 0.1 * state[0]
    total[...] = update
    u_sums = piece_sums(update * update, position, starts)

    stat_z[z, 0:1, :] = w_sums
    stat_z[z, 1:2, :] = u_sums

    def n_copy(o):
        zz = (z + o) % NZ
        return pltpu.make_async_remote_copy(
            src_ref=stat_z.at[z, pl.ds(0, 2)], dst_ref=stat_z.at[z, pl.ds(0, 2)],
            send_sem=ns_sem.at[o], recv_sem=nr_sem.at[z],
            device_id=at(zz, x, t), device_id_type=MESH,
        )

    def n_arrival(o):
        zz = (z + o) % NZ
        return pltpu.make_async_remote_copy(
            src_ref=stat_z.at[z, pl.ds(0, 2)], dst_ref=stat_z.at[zz, pl.ds(0, 2)],
            send_sem=ns_sem.at[o], recv_sem=nr_sem.at[zz],
            device_id=at(zz, x, t), device_id_type=MESH,
        )

    for o in (8, 7, 9, 6, 10, 5, 11, 4, 12, 3, 13, 2, 14, 1, 15):
        n_copy(o).start()
    for o in range(1, NZ):
        n_arrival(o).wait_recv()
    sums = stat_z[0, 0:2, :]
    for zz in range(1, NZ):
        sums = sums + stat_z[zz, 0:2, :]
    me = x * NT + t
    stat_p[me, 0:2, :] = sums

    plane = [
        (dx, dy, dc) for dx in (2, 1, 3, 0) for dy in (2, 1, 3, 0) for dc in (1, 0) if dx or dy or dc
    ]

    def p_copy(n):
        return pltpu.make_async_remote_copy(
            src_ref=stat_p.at[me, pl.ds(0, 2)], dst_ref=stat_p.at[me, pl.ds(0, 2)],
            send_sem=ps_sem.at[n], recv_sem=pr_sem.at[me],
            device_id=near(*plane[n]), device_id_type=MESH,
        )

    def p_arrival(n):
        dp_there, t_there = near(*plane[n])
        slot = (dp_there - z * NX) * NT + t_there
        return pltpu.make_async_remote_copy(
            src_ref=stat_p.at[me, pl.ds(0, 2)], dst_ref=stat_p.at[slot, pl.ds(0, 2)],
            send_sem=ps_sem.at[n], recv_sem=pr_sem.at[slot],
            device_id=near(*plane[n]), device_id_type=MESH,
        )

    for n in range(NX * NT - 1):
        p_copy(n).start()
    for n in range(NX * NT - 1):
        p_arrival(n).wait_recv()
    data_sum = stat_p[t, 0:2, :]
    for xx in range(1, NX):
        data_sum = data_sum + stat_p[xx * NT + t, 0:2, :]
    tensor_sum = stat_p[0, 0:2, :]
    for i in range(1, NX * NT):
        tensor_sum = tensor_sum + stat_p[i, 0:2, :]
    effective = jnp.where(split == 1, tensor_sum, data_sum)
    trust = jnp.sqrt(effective[0:1]) / jnp.maximum(jnp.sqrt(effective[1:2]), 1.0)
    trust_at = jnp.broadcast_to(trust[:, 0:1], (ROWS, 128))
    for k in range(1, NP):
        trust_at = jnp.where(position >= starts[k], trust[:, k : k + 1], trust_at)
    new_weights = state[0] - 0.05 * trust_at * total[...]

    weights[z, x] = new_weights.astype(jnp.bfloat16)

    def g_copy(back, o):
        block = weights.at[(z - back) % NZ, x]
        return pltpu.make_async_remote_copy(
            src_ref=block, dst_ref=block,
            send_sem=gs_sem.at[back, o], recv_sem=gr_sem.at[(z - back) % NZ],
            device_id=at((z + o) % NZ, x, t), device_id_type=MESH,
        )

    def f_copy(back, dx):
        block = weights.at[(z - back) % NZ, x]
        return pltpu.make_async_remote_copy(
            src_ref=block, dst_ref=block,
            send_sem=fs_sem.at[back, dx], recv_sem=fr_sem.at[x, (z - back) % NZ],
            device_id=at(z, (x + dx) % NX, t), device_id_type=MESH,
        )

    def f_arrival(back, dx):
        xx = (x + dx) % NX
        block = weights.at[(z - back) % NZ, xx]
        return pltpu.make_async_remote_copy(
            src_ref=block, dst_ref=block,
            send_sem=fs_sem.at[back, dx], recv_sem=fr_sem.at[xx, (z - back) % NZ],
            device_id=at(z, xx, t), device_id_type=MESH,
        )

    def relay(back):
        for o in SHORT:
            g_copy(back, o).start()

    def spread(back):
        for dx in (2, 1, 3):
            f_copy(back, dx).start()

    for o in LONG:
        g_copy(0, o).start()
    relay(0)
    spread(0)
    made[0] = new_weights
    out_copies[0].start()

    for back in ARRIVALS:
        g_copy(back, 1).wait_recv()
        if back in LONG:
            relay(back)
        spread(back)
    for back in (0, *ARRIVALS):
        for dx in (1, 3, 2):
            f_arrival(back, dx).wait_recv()

    for copy in out_copies:
        copy.wait()
    for k in ORDER:
        for o in range(1, NX):
            x_copy(k, o).wait_send()
    for o in range(1, NZ):
        z_copy((z + o) % NZ).wait_send()
        n_copy(o).wait_send()
    for n in range(NX * NT - 1):
        p_copy(n).wait_send()
    for o in LONG:
        g_copy(0, o).wait_send()
    for back in (0, *LONG):
        for o in SHORT:
            g_copy(back, o).wait_send()
    for back in range(NZ):
        for dx in range(1, NX):
            f_copy(back, dx).wait_send()


def local(grads, piece_lengths, split_flags, master_params, exp_avg, exp_avg_sq):
    vmem = pl.BlockSpec(memory_space=pltpu.VMEM)
    anywhere = pl.BlockSpec(memory_space=pltpu.HBM)
    shard = jax.ShapeDtypeStruct((ROWS, 128), jnp.float32)
    dma = pltpu.SemaphoreType.DMA
    hbm = lambda array: pltpu.with_memory_space_constraint(array, pltpu.HBM)
    new_master, new_avg, new_avg_sq, model = pl.pallas_call(
        kernel,
        name="lamb",
        out_shape=(shard, shard, shard, jax.ShapeDtypeStruct((NZ, NX, ROWS, 128), jnp.bfloat16)),
        in_specs=[anywhere] * 6,
        out_specs=(anywhere, anywhere, anywhere, vmem),
        scratch_shapes=[
            pltpu.VMEM((NZ * NX * ROWS, 128), jnp.float32),
            pltpu.VMEM((NX, GROUP, XROWS, 128), jnp.int32),
            pltpu.VMEM((NX, GROUP, XROWS, 128), jnp.int32),
            pltpu.VMEM((NZ, WORDS + 8, 128), jnp.int32),
            pltpu.VMEM((NZ, WORDS + 8, 128), jnp.int32),
            pltpu.VMEM((ROWS, 128), jnp.float32),
            pltpu.VMEM((3, ROWS, 128), jnp.float32),
            pltpu.VMEM((3, ROWS, 128), jnp.float32),
            pltpu.VMEM((NZ, 8, 128), jnp.float32),
            pltpu.VMEM((NX * NT, 8, 128), jnp.float32),
            pltpu.SMEM((NP,), jnp.int32),
            pltpu.SMEM((NP,), jnp.int32),
            pltpu.SemaphoreType.REGULAR((3,)), dma((4,)), dma((5,)), dma((3,)),
            dma((NX, 4)), dma((NX, 4)),
            dma((NZ,)), dma((NZ,)),
            dma((NZ,)), dma((NZ,)),
            dma((NX * NT,)), dma((NX * NT,)),
            dma((NZ, NZ)), dma((NZ,)),
            dma((NZ, NX)), dma((NX, NZ)),
        ],
        compiler_params=pltpu.CompilerParams(
            collective_id=0, has_side_effects=True, vmem_limit_bytes=24 * 2**20
        ),
    )(
        hbm(piece_lengths), hbm(split_flags), hbm(grads.reshape(NZ * NX * ROWS, 128)),
        hbm(master_params.reshape(ROWS, 128)), hbm(exp_avg.reshape(ROWS, 128)), hbm(exp_avg_sq.reshape(ROWS, 128)),
    )
    model = lax.optimization_barrier(model.reshape(-1))
    return (
        new_master.reshape(1, -1), new_avg.reshape(1, -1), new_avg_sq.reshape(1, -1), model.reshape(1, -1)
    )


def solution(mesh):
    return jax.shard_map(
        local,
        mesh=mesh,
        in_specs=(
            P("dp", "tensor", None),
            P(),
            P(),
            P("tensor", "dp"),
            P("tensor", "dp"),
            P("tensor", "dp"),
        ),
        out_specs=(P("tensor", "dp"), P("tensor", "dp"), P("tensor", "dp"), P("tensor", None)),
        check_vma=False,
    )
```

```python
import jax
import jax.numpy as jnp
from jax import lax
from jax.experimental import pallas as pl
from jax.experimental.pallas import tpu as pltpu
from jax.sharding import PartitionSpec as P

MESH = pl.DeviceIdType.MESH
NZ, NX, NY, NT = 16, 4, 4, 8
ROWS = 64
WORDS = 32
NP = 40
CODED = WORDS + 1


def encode(block, unit):
    top = jnp.max(jnp.abs(block), axis=0, keepdims=True)
    scale = (top * unit).astype(jnp.int32) + 1
    inverse = (32767.0 * unit) / scale.astype(jnp.float32)
    codes = jnp.round(block * inverse).astype(jnp.int32)
    return (codes[:WORDS] << 16) + codes[WORDS:], scale


def decode(words, scale, unit):
    step = scale.astype(jnp.float32) * (1.0 / (32767.0 * unit))
    high = ((words + 32768) >> 16).astype(jnp.float32) * step
    low = ((words << 16) >> 16).astype(jnp.float32) * step
    return high, low


NEAR = (2, 14, 1, 15)
LONG = (8, 5, 11, 3, 13)
RELAYS = {3: (1,), 13: (15,), 5: (2, 1), 11: (14, 15), 8: ()}
ARRIVALS = (3, 13, 5, 11, 4, 12, 8, 6, 10, 7, 9)
FAR_FIRST = (8, 7, 9, 6, 10, 5, 11, 4, 12, 3, 13, 2, 14, 1, 15)

UNIT_X = float(2**26)
UNIT_Z = float(2**24)


def piece_sums(values, position, starts):
    rows = []
    for k in range(NP):
        inside = (position >= starts[k]) & (position < starts[k + 1])
        rows.append(jnp.sum(jnp.where(inside, values, 0.0), axis=0, keepdims=True))
    table = jnp.concatenate(rows, axis=0)
    totals = jnp.sum(table, axis=1, keepdims=True)
    piece = lax.broadcasted_iota(jnp.int32, (NP, 128), 0)
    lane = lax.broadcasted_iota(jnp.int32, (NP, 128), 1)
    return jnp.sum(jnp.where(piece == lane, totals, 0.0), axis=0, keepdims=True)


def kernel(
    lengths_in, flags_in, grads, master, avg, avg_sq,
    made, weights,
    held, coded, x_in, z_out, z_in, total, state, stat_z, stat_p, lengths, flags,
    word_sem, load_sem, state_sem, xs_sem, xr_sem, zs_sem, zr_sem, ns_sem, nr_sem, ps_sem, pr_sem,
    gs_sem, gr_sem, rs_sem, rr_sem, fs_sem, fr_sem,
):
    dp = lax.axis_index("dp")
    t = lax.axis_index("tensor")
    z, x = dp // NX, dp % NX

    def at(zz, xx, tt):
        return (zz * NX + xx, tt)

    def load(zz):
        rows = pl.ds(pl.multiple_of(zz * (NX * ROWS), NX * ROWS), NX * ROWS)
        return pltpu.make_async_copy(grads.at[rows], held.at[rows], load_sem.at[zz])

    for o in (*FAR_FIRST, 0):
        load((z + o) % NZ).start()
    state_copies = [
        pltpu.make_async_copy(ref, state.at[i], state_sem.at[i])
        for i, ref in enumerate((master, avg, avg_sq))
    ]
    state_copies += [
        pltpu.make_async_copy(lengths_in, lengths, state_sem.at[3]),
        pltpu.make_async_copy(flags_in, flags, state_sem.at[4]),
    ]
    for copy in state_copies:
        copy.start()

    barrier = pltpu.get_barrier_semaphore()

    y, core = t // 2, t % 2

    def near(dx, dy, dc):
        return at(z, (x + dx) % NX, ((y + dy) % NY) * 2 + (core + dc) % 2)

    greeted = [near(dx, 0, 0) for dx in range(1, NX)]
    greeted += [near(0, dy, dc) for dy in range(NY) for dc in range(2) if dy or dc]
    greeted += [at((z + o) % NZ, x, t) for o in (1, 15, 2, 14, 3, 13, 4, 12)]
    for device in greeted:
        pl.semaphore_signal(barrier, 1, device_id=device, device_id_type=MESH)

    def far(i):
        return jnp.where(i % 2 == 0, NZ // 2 + i // 2, NZ // 2 - (i + 1) // 2)

    def x_copy(zz, dx):
        xx = (x + dx) % NX
        return pltpu.make_async_remote_copy(
            src_ref=coded.at[xx, zz, pl.ds(0, CODED)], dst_ref=x_in.at[x, zz, pl.ds(0, CODED)],
            send_sem=xs_sem.at[dx, zz], recv_sem=xr_sem.at[x, zz],
            device_id=at(z, xx, t), device_id_type=MESH,
        )

    def x_arrival(zz, dx):
        xx = (x + dx) % NX
        return pltpu.make_async_remote_copy(
            src_ref=coded.at[xx, zz, pl.ds(0, CODED)], dst_ref=x_in.at[xx, zz, pl.ds(0, CODED)],
            send_sem=xs_sem.at[dx, zz], recv_sem=xr_sem.at[xx, zz],
            device_id=at(z, xx, t), device_id_type=MESH,
        )

    pl.semaphore_wait(barrier, len(greeted))
    for o in (4, 12):
        pl.semaphore_signal(word_sem, 1, device_id=at((z + o) % NZ, x, t), device_id_type=MESH)

    def scatter(i, c):
        zz = (z + far(i)) % NZ
        load(zz).wait()
        for dx in (2, 1, 3):
            xx = (x + dx) % NX
            start = pl.multiple_of((zz * NX + xx) * ROWS, ROWS)
            words, scale = encode(held[pl.ds(start, ROWS), :], UNIT_X)
            coded[xx, zz, :WORDS, :] = words
            coded[xx, zz, WORDS:CODED, :] = scale
            x_copy(zz, dx).start()
        return c

    lax.fori_loop(0, NZ, scatter, 0)

    for copy in state_copies:
        copy.wait()
    starts = [jnp.int32(0)]
    split = jnp.zeros((1, 128), jnp.int32)
    for k in range(NP):
        starts.append(starts[-1] + lengths[k])
        split = jnp.where(lax.broadcasted_iota(jnp.int32, (1, 128), 1) == k, flags[k], split)
    position = (
        dp * (ROWS * 128)
        + lax.broadcasted_iota(jnp.int32, (ROWS, 128), 0) * 128
        + lax.broadcasted_iota(jnp.int32, (ROWS, 128), 1)
    )
    w = state[0]
    w_sums = piece_sums(w * w, position, starts)

    def z_copy(zz):
        return pltpu.make_async_remote_copy(
            src_ref=z_out.at[zz, pl.ds(0, CODED)], dst_ref=z_in.at[z, pl.ds(0, CODED)],
            send_sem=zs_sem.at[zz], recv_sem=zr_sem.at[z],
            device_id=at(zz, x, t), device_id_type=MESH,
        )

    def z_arrival(zz):
        return pltpu.make_async_remote_copy(
            src_ref=z_out.at[zz, pl.ds(0, CODED)], dst_ref=z_in.at[zz, pl.ds(0, CODED)],
            send_sem=zs_sem.at[zz], recv_sem=zr_sem.at[zz],
            device_id=at(zz, x, t), device_id_type=MESH,
        )

    def sum_over_x(zz):
        start = pl.multiple_of((zz * NX + x) * ROWS, ROWS)
        high = held[pl.ds(start, WORDS), :]
        low = held[pl.ds(pl.multiple_of(start + WORDS, WORDS), WORDS), :]
        for dx in (1, 3, 2):
            xx = (x + dx) % NX
            x_arrival(zz, dx).wait_recv()
            h, l = decode(x_in[xx, zz, :WORDS, :], x_in[xx, zz, WORDS:CODED, :], UNIT_X)
            high, low = high + h, low + l
        return high, low

    def forward(i, c):
        zz = (z + far(i)) % NZ
        high, low = sum_over_x(zz)
        words, scale = encode(jnp.concatenate([high, low], axis=0), UNIT_Z)
        z_out[zz, :WORDS, :] = words
        z_out[zz, WORDS:CODED, :] = scale
        z_copy(zz).start()
        return c

    pl.semaphore_wait(word_sem, 2)
    lax.fori_loop(0, NZ - 1, forward, 0)
    high, low = sum_over_x(z)
    total[:WORDS, :] = high
    total[WORDS:, :] = low

    def collect(o, c):
        zz = (z + o) % NZ
        z_arrival(zz).wait_recv()
        h, l = decode(z_in[zz, :WORDS, :], z_in[zz, WORDS:CODED, :], UNIT_Z)
        total[:WORDS, :] += h
        total[WORDS:, :] += l
        return c

    lax.fori_loop(1, NZ, collect, 0)

    grad = total[...] * (1.0 / (NZ * NX))
    new_avg = 0.9 * state[1] + 0.1 * grad
    new_avg_sq = 0.95 * state[2] + 0.05 * grad * grad
    made[1] = new_avg
    made[2] = new_avg_sq
    update = new_avg / (jnp.sqrt(new_avg_sq) + 1e-08) + 0.1 * state[0]
    total[...] = update
    u_sums = piece_sums(update * update, position, starts)

    mine = z * 2 + core
    stat_z[mine, 0:1, :] = w_sums
    stat_z[mine, 1:2, :] = u_sums
    line = [(o, dc) for o in FAR_FIRST for dc in (1, 0)] + [(0, 1)]

    def n_copy(n, slot=mine):
        o, dc = line[n]
        return pltpu.make_async_remote_copy(
            src_ref=stat_z.at[mine, pl.ds(0, 2)], dst_ref=stat_z.at[slot, pl.ds(0, 2)],
            send_sem=ns_sem.at[n], recv_sem=nr_sem.at[slot],
            device_id=at((z + o) % NZ, x, y * 2 + (core + dc) % 2), device_id_type=MESH,
        )

    def n_arrival(n):
        o, dc = line[n]
        return n_copy(n, ((z + o) % NZ) * 2 + (core + dc) % 2)

    for n in range(len(line)):
        n_copy(n).start()
    for n in reversed(range(len(line))):
        n_arrival(n).wait_recv()
    own = stat_z[core, 0:2, :]
    other = stat_z[1 - core, 0:2, :]
    for zz in range(1, NZ):
        own = own + stat_z[zz * 2 + core, 0:2, :]
        other = other + stat_z[zz * 2 + 1 - core, 0:2, :]
    me = x * NY + y
    stat_p[me, 0:2, :] = own
    stat_p[me, 2:4, :] = own + other
    plane = [(dx, dy) for dx in (2, 1, 3, 0) for dy in (2, 1, 3, 0) if dx or dy]

    def p_copy(n, slot=me):
        dx, dy = plane[n]
        return pltpu.make_async_remote_copy(
            src_ref=stat_p.at[me, pl.ds(0, 4)], dst_ref=stat_p.at[slot, pl.ds(0, 4)],
            send_sem=ps_sem.at[n], recv_sem=pr_sem.at[slot],
            device_id=near(dx, dy, 0), device_id_type=MESH,
        )

    def p_arrival(n):
        dx, dy = plane[n]
        return p_copy(n, ((x + dx) % NX) * NY + (y + dy) % NY)

    for n in range(len(plane)):
        p_copy(n).start()
    for n in reversed(range(len(plane))):
        p_arrival(n).wait_recv()
    data_sum = stat_p[y, 0:2, :]
    for xx in range(1, NX):
        data_sum = data_sum + stat_p[xx * NY + y, 0:2, :]
    tensor_sum = stat_p[0, 2:4, :]
    for i in range(1, NX * NY):
        tensor_sum = tensor_sum + stat_p[i, 2:4, :]
    effective = jnp.where(split == 1, tensor_sum, data_sum)
    trust = jnp.sqrt(effective[0:1]) / jnp.maximum(jnp.sqrt(effective[1:2]), 1.0)
    trust_at = jnp.broadcast_to(trust[:, 0:1], (ROWS, 128))
    for k in range(1, NP):
        trust_at = jnp.where(position >= starts[k], trust[:, k : k + 1], trust_at)
    new_weights = state[0] - 0.05 * trust_at * total[...]

    weights[z, x] = new_weights.astype(jnp.bfloat16)

    def g_copy(back, o):
        block = weights.at[(z - back) % NZ, x]
        return pltpu.make_async_remote_copy(
            src_ref=block, dst_ref=block,
            send_sem=gs_sem.at[back, o], recv_sem=gr_sem.at[(z - back) % NZ],
            device_id=at((z + o) % NZ, x, t), device_id_type=MESH,
        )

    def f_copy(back, dx):
        block = weights.at[(z - back) % NZ, x]
        return pltpu.make_async_remote_copy(
            src_ref=block, dst_ref=block,
            send_sem=fs_sem.at[back, dx], recv_sem=fr_sem.at[x, (z - back) % NZ],
            device_id=at(z, (x + dx) % NX, t), device_id_type=MESH,
        )

    def f_arrival(back, dx):
        xx = (x + dx) % NX
        block = weights.at[(z - back) % NZ, xx]
        return pltpu.make_async_remote_copy(
            src_ref=block, dst_ref=block,
            send_sem=fs_sem.at[back, dx], recv_sem=fr_sem.at[xx, (z - back) % NZ],
            device_id=at(z, xx, t), device_id_type=MESH,
        )

    def r_copy(o, row=z):
        return pltpu.make_async_remote_copy(
            src_ref=weights.at[row], dst_ref=weights.at[row],
            send_sem=rs_sem.at[o], recv_sem=rr_sem.at[row],
            device_id=at((z + o) % NZ, x, t), device_id_type=MESH,
        )

    def spread(back):
        for dx in (2, 1, 3):
            f_copy(back, dx).start()

    for o in LONG:
        g_copy(0, o).start()
    spread(0)
    made[0] = new_weights

    for o in range(1, NZ):
        for dx in range(1, NX):
            x_copy((z + o) % NZ, dx).wait_send()
        z_copy((z + o) % NZ).wait_send()
    for dx in range(1, NX):
        x_copy(z, dx).wait_send()
    for n in range(len(line)):
        n_copy(n).wait_send()
    for n in range(len(plane)):
        p_copy(n).wait_send()

    for back in ARRIVALS:
        g_copy(back, 1).wait_recv()
        for o in RELAYS.get(back, ()):
            g_copy(back, o).start()
        spread(back)
        if back == 11:
            for dx in (1, 3, 2):
                f_arrival(0, dx).wait_recv()
            for o in NEAR:
                r_copy(o).start()
    for o in NEAR:
        r_copy(o, (z + o) % NZ).wait_recv()
    for back in ARRIVALS:
        for dx in (1, 3, 2):
            f_arrival(back, dx).wait_recv()

    for o in NEAR:
        r_copy(o).wait_send()
    for o in LONG:
        g_copy(0, o).wait_send()
        for far_o in RELAYS[o]:
            g_copy(o, far_o).wait_send()
    for back in (0, *ARRIVALS):
        for dx in range(1, NX):
            f_copy(back, dx).wait_send()


def local(grads, piece_lengths, split_flags, master_params, exp_avg, exp_avg_sq):
    vmem = pl.BlockSpec(memory_space=pltpu.VMEM)
    anywhere = pl.BlockSpec(memory_space=pltpu.HBM)
    dma = pltpu.SemaphoreType.DMA
    hbm = lambda array: pltpu.with_memory_space_constraint(array, pltpu.HBM)
    made, model = pl.pallas_call(
        kernel,
        name="lamb",
        out_shape=(jax.ShapeDtypeStruct((3, ROWS, 128), jnp.float32), jax.ShapeDtypeStruct((NZ, NX, ROWS, 128), jnp.bfloat16)),
        in_specs=[anywhere] * 6,
        out_specs=(vmem, vmem),
        scratch_shapes=[
            pltpu.VMEM((NZ * NX * ROWS, 128), jnp.float32),
            pltpu.VMEM((NX, NZ, WORDS + 8, 128), jnp.int32),
            pltpu.VMEM((NX, NZ, WORDS + 8, 128), jnp.int32),
            pltpu.VMEM((NZ, WORDS + 8, 128), jnp.int32),
            pltpu.VMEM((NZ, WORDS + 8, 128), jnp.int32),
            pltpu.VMEM((ROWS, 128), jnp.float32),
            pltpu.VMEM((3, ROWS, 128), jnp.float32),
            pltpu.VMEM((NZ * 2, 8, 128), jnp.float32),
            pltpu.VMEM((NX * NY, 8, 128), jnp.float32),
            pltpu.SMEM((NP,), jnp.int32),
            pltpu.SMEM((NP,), jnp.int32),
            pltpu.SemaphoreType.REGULAR, dma((NZ,)), dma((5,)),
            dma((NX, NZ)), dma((NX, NZ)),
            dma((NZ,)), dma((NZ,)),
            dma((NZ * 2,)), dma((NZ * 2,)),
            dma((NX * NY,)), dma((NX * NY,)),
            dma((NZ, NZ)), dma((NZ,)),
            dma((NZ,)), dma((NZ,)),
            dma((NZ, NX)), dma((NX, NZ)),
        ],
        compiler_params=pltpu.CompilerParams(
            collective_id=0, has_side_effects=True, vmem_limit_bytes=24 * 2**20
        ),
    )(
        hbm(piece_lengths), hbm(split_flags), hbm(grads.reshape(NZ * NX * ROWS, 128)),
        hbm(master_params.reshape(ROWS, 128)), hbm(exp_avg.reshape(ROWS, 128)), hbm(exp_avg_sq.reshape(ROWS, 128)),
    )
    model = lax.optimization_barrier(model.reshape(-1))
    return (
        made[0].reshape(1, -1), made[1].reshape(1, -1), made[2].reshape(1, -1), model.reshape(1, -1)
    )


def solution(mesh):
    return jax.shard_map(
        local,
        mesh=mesh,
        in_specs=(
            P("dp", "tensor", None),
            P(),
            P(),
            P("tensor", "dp"),
            P("tensor", "dp"),
            P("tensor", "dp"),
        ),
        out_specs=(P("tensor", "dp"), P("tensor", "dp"), P("tensor", "dp"), P("tensor", None)),
        check_vma=False,
    )
```

```python
import jax
import jax.numpy as jnp
from jax import lax
from jax.experimental import pallas as pl
from jax.experimental.pallas import tpu as pltpu
from jax.sharding import PartitionSpec as P

MESH = pl.DeviceIdType.MESH
NZ, NX, NY, NT = 16, 4, 4, 8
ROWS = 64
WORDS = 32
NP = 40
CODED = WORDS + 1


def encode(block, unit):
    top = jnp.max(jnp.abs(block), axis=0, keepdims=True)
    scale = (top * unit).astype(jnp.int32) + 1
    inverse = (32767.0 * unit) / scale.astype(jnp.float32)
    codes = jnp.round(block * inverse).astype(jnp.int32)
    return (codes[:WORDS] << 16) + codes[WORDS:], scale


def decode(words, scale, unit):
    step = scale.astype(jnp.float32) * (1.0 / (32767.0 * unit))
    high = ((words + 32768) >> 16).astype(jnp.float32) * step
    low = ((words << 16) >> 16).astype(jnp.float32) * step
    return high, low


NEAR = (2, 14, 1, 15)
LONG = (8, 5, 11, 3, 13)
RELAYS = {3: (1,), 13: (15,), 5: (2, 1), 11: (14, 15), 8: ()}
ARRIVALS = (3, 13, 5, 11, 4, 12, 8, 6, 10, 7, 9)
FAR_FIRST = (8, 7, 9, 6, 10, 5, 11, 4, 12, 3, 13, 2, 14, 1, 15)

UNIT_X = float(2**26)
UNIT_Z = float(2**24)


def piece_sums(values, position, starts, first):
    rows = []
    for k in range(NP):
        inside = (position >= starts[k]) & (position < starts[k + 1])
        rows.append(jnp.sum(jnp.where(inside, values, 0.0), axis=0, keepdims=True))
    table = jnp.concatenate(rows, axis=0)
    totals = jnp.sum(table, axis=1, keepdims=True)
    piece = lax.broadcasted_iota(jnp.int32, (NP, 128), 0)
    lane = lax.broadcasted_iota(jnp.int32, (NP, 128), 1)
    return jnp.sum(jnp.where(piece + first == lane, totals, 0.0), axis=0, keepdims=True)


def kernel(
    lengths_in, flags_in, grads, master, avg, avg_sq,
    made, weights,
    held, coded, x_in, z_out, z_in, total, state, stat_z, stat_p, lengths, flags,
    word_sem, load_sem, state_sem, send_sem, land_sem, xr_sem, gr_sem,
):
    dp = lax.axis_index("dp")
    t = lax.axis_index("tensor")
    z, x = dp // NX, dp % NX

    def at(zz, xx, tt):
        return (zz * NX + xx, tt)

    def landed(ref, sem):
        pltpu.make_async_remote_copy(
            src_ref=ref, dst_ref=ref, send_sem=sem, recv_sem=sem,
            device_id=at(z, (x + 1) % NX, t), device_id_type=MESH,
        ).wait_recv()

    def gone(ref, sem):
        pltpu.make_async_remote_copy(
            src_ref=ref, dst_ref=ref, send_sem=sem, recv_sem=sem,
            device_id=at(z, (x + 1) % NX, t), device_id_type=MESH,
        ).wait_send()

    def load(zz):
        rows = pl.ds(pl.multiple_of(zz * (NX * ROWS), NX * ROWS), NX * ROWS)
        return pltpu.make_async_copy(grads.at[rows], held.at[rows], load_sem.at[zz])

    for o in (*FAR_FIRST, 0):
        load((z + o) % NZ).start()
    for i, ref in enumerate((master, avg, avg_sq)):
        pltpu.make_async_copy(ref, state.at[i], state_sem.at[0]).start()
    tables = [
        pltpu.make_async_copy(lengths_in, lengths, state_sem.at[1]),
        pltpu.make_async_copy(flags_in, flags, state_sem.at[2]),
    ]
    for copy in tables:
        copy.start()

    barrier = pltpu.get_barrier_semaphore()

    y, core = t // 2, t % 2

    def near(dx, dy, dc):
        return at(z, (x + dx) % NX, ((y + dy) % NY) * 2 + (core + dc) % 2)

    greeted = [near(dx, 0, 0) for dx in range(1, NX)]
    greeted += [near(0, dy, dc) for dy in range(NY) for dc in range(2) if dy or dc]
    greeted += [at((z + o) % NZ, x, t) for o in (1, 15, 2, 14, 3, 13, 4, 12)]
    for device in greeted:
        pl.semaphore_signal(barrier, 1, device_id=device, device_id_type=MESH)

    def far(i):
        return jnp.where(i % 2 == 0, NZ // 2 + i // 2, NZ // 2 - (i + 1) // 2)

    def x_copy(zz, dx):
        xx = (x + dx) % NX
        return pltpu.make_async_remote_copy(
            src_ref=coded.at[xx, zz, pl.ds(0, CODED)], dst_ref=x_in.at[x, zz, pl.ds(0, CODED)],
            send_sem=send_sem.at[0], recv_sem=xr_sem.at[zz],
            device_id=at(z, xx, t), device_id_type=MESH,
        )

    pl.semaphore_wait(barrier, len(greeted))
    for o in (4, 12):
        pl.semaphore_signal(word_sem, 1, device_id=at((z + o) % NZ, x, t), device_id_type=MESH)

    def scatter(i, c):
        zz = (z + far(i)) % NZ
        load(zz).wait()
        for dx in (2, 1, 3):
            xx = (x + dx) % NX
            start = pl.multiple_of((zz * NX + xx) * ROWS, ROWS)
            words, scale = encode(held[pl.ds(start, ROWS), :], UNIT_X)
            coded[xx, zz, :WORDS, :] = words
            coded[xx, zz, WORDS:CODED, :] = scale
            x_copy(zz, dx).start()
        return c

    lax.fori_loop(0, NZ, scatter, 0)

    for copy in tables:
        copy.wait()
    pltpu.make_async_copy(state, state, state_sem.at[0]).wait()
    starts = [jnp.int32(0)]
    split = jnp.zeros((1, 128), jnp.int32)
    lane = lax.broadcasted_iota(jnp.int32, (1, 128), 1)
    for k in range(NP):
        starts.append(starts[-1] + lengths[k])
        split = jnp.where((lane == k) | (lane == k + 64), flags[k], split)
    position = (
        dp * (ROWS * 128)
        + lax.broadcasted_iota(jnp.int32, (ROWS, 128), 0) * 128
        + lax.broadcasted_iota(jnp.int32, (ROWS, 128), 1)
    )
    w = state[0]
    w_sums = piece_sums(w * w, position, starts, 0)

    def z_copy(zz):
        return pltpu.make_async_remote_copy(
            src_ref=z_out.at[zz, pl.ds(0, CODED)], dst_ref=z_in.at[z, pl.ds(0, CODED)],
            send_sem=send_sem.at[1], recv_sem=land_sem.at[0],
            device_id=at(zz, x, t), device_id_type=MESH,
        )

    def sum_over_x(zz):
        start = pl.multiple_of((zz * NX + x) * ROWS, ROWS)
        high = held[pl.ds(start, WORDS), :]
        low = held[pl.ds(pl.multiple_of(start + WORDS, WORDS), WORDS), :]
        landed(x_in.at[pl.ds(0, NX - 1), zz, pl.ds(0, CODED)], xr_sem.at[zz])
        for dx in (1, 3, 2):
            xx = (x + dx) % NX
            h, l = decode(x_in[xx, zz, :WORDS, :], x_in[xx, zz, WORDS:CODED, :], UNIT_X)
            high, low = high + h, low + l
        return high, low

    def forward(i, c):
        zz = (z + far(i)) % NZ
        high, low = sum_over_x(zz)
        words, scale = encode(jnp.concatenate([high, low], axis=0), UNIT_Z)
        z_out[zz, :WORDS, :] = words
        z_out[zz, WORDS:CODED, :] = scale
        z_copy(zz).start()
        return c

    pl.semaphore_wait(word_sem, 2)
    lax.fori_loop(0, NZ - 1, forward, 0)
    high, low = sum_over_x(z)
    total[:WORDS, :] = high
    total[WORDS:, :] = low

    landed(z_in.at[pl.ds(0, NZ - 1), pl.ds(0, CODED)], land_sem.at[0])

    def collect(o, c):
        zz = (z + o) % NZ
        h, l = decode(z_in[zz, :WORDS, :], z_in[zz, WORDS:CODED, :], UNIT_Z)
        total[:WORDS, :] += h
        total[WORDS:, :] += l
        return c

    lax.fori_loop(1, NZ, collect, 0)

    grad = total[...] * (1.0 / (NZ * NX))
    new_avg = 0.9 * state[1] + 0.1 * grad
    new_avg_sq = 0.95 * state[2] + 0.05 * grad * grad
    made[1] = new_avg
    made[2] = new_avg_sq
    update = new_avg / (jnp.sqrt(new_avg_sq) + 1e-08) + 0.1 * state[0]
    total[...] = update
    u_sums = piece_sums(update * update, position, starts, 64)

    mine = z * 2 + core
    stat_z[mine, 0:1, :] = w_sums + u_sums
    line = [(o, dc) for o in FAR_FIRST for dc in (1, 0)] + [(0, 1)]
    for o, dc in line:
        pltpu.make_async_remote_copy(
            src_ref=stat_z.at[mine, pl.ds(0, 1)], dst_ref=stat_z.at[mine, pl.ds(0, 1)],
            send_sem=send_sem.at[2], recv_sem=land_sem.at[1],
            device_id=at((z + o) % NZ, x, y * 2 + (core + dc) % 2), device_id_type=MESH,
        ).start()
    landed(stat_z.at[pl.ds(0, len(line)), pl.ds(0, 1)], land_sem.at[1])
    own = stat_z[core, 0:1, :]
    other = stat_z[1 - core, 0:1, :]
    for zz in range(1, NZ):
        own = own + stat_z[zz * 2 + core, 0:1, :]
        other = other + stat_z[zz * 2 + 1 - core, 0:1, :]
    me = x * NY + y
    stat_p[me, 0:1, :] = own
    stat_p[me, 1:2, :] = own + other
    plane = [(dx, dy) for dx in (2, 1, 3, 0) for dy in (2, 1, 3, 0) if dx or dy]
    for dx, dy in plane:
        pltpu.make_async_remote_copy(
            src_ref=stat_p.at[me, pl.ds(0, 2)], dst_ref=stat_p.at[me, pl.ds(0, 2)],
            send_sem=send_sem.at[3], recv_sem=land_sem.at[2],
            device_id=near(dx, dy, 0), device_id_type=MESH,
        ).start()
    landed(stat_p.at[pl.ds(0, len(plane)), pl.ds(0, 2)], land_sem.at[2])
    data_sum = stat_p[y, 0:1, :]
    for xx in range(1, NX):
        data_sum = data_sum + stat_p[xx * NY + y, 0:1, :]
    tensor_sum = stat_p[0, 1:2, :]
    for i in range(1, NX * NY):
        tensor_sum = tensor_sum + stat_p[i, 1:2, :]
    effective = jnp.where(split == 1, tensor_sum, data_sum)
    norms = jnp.sqrt(effective)
    trust = norms / jnp.maximum(pltpu.roll(norms, 64, 1), 1.0)
    trust_at = jnp.broadcast_to(trust[:, 0:1], (ROWS, 128))
    for k in range(1, NP):
        trust_at = jnp.where(position >= starts[k], trust[:, k : k + 1], trust_at)
    new_weights = state[0] - 0.05 * trust_at * total[...]

    weights[z, x] = new_weights.astype(jnp.bfloat16)

    def g_copy(back, o):
        block = weights.at[(z - back) % NZ, x]
        return pltpu.make_async_remote_copy(
            src_ref=block, dst_ref=block,
            send_sem=send_sem.at[4], recv_sem=gr_sem.at[(back + o) % NZ],
            device_id=at((z + o) % NZ, x, t), device_id_type=MESH,
        )

    def f_copy(back, dx):
        block = weights.at[(z - back) % NZ, x]
        return pltpu.make_async_remote_copy(
            src_ref=block, dst_ref=block,
            send_sem=send_sem.at[5], recv_sem=land_sem.at[4 if back else 3],
            device_id=at(z, (x + dx) % NX, t), device_id_type=MESH,
        )

    def r_copy(o):
        return pltpu.make_async_remote_copy(
            src_ref=weights.at[z], dst_ref=weights.at[z],
            send_sem=send_sem.at[6], recv_sem=land_sem.at[5],
            device_id=at((z + o) % NZ, x, t), device_id_type=MESH,
        )

    def spread(back):
        for dx in (2, 1, 3):
            f_copy(back, dx).start()

    for o in LONG:
        g_copy(0, o).start()
    spread(0)
    made[0] = new_weights

    gone(coded.at[pl.ds(0, NX - 1), :, pl.ds(0, CODED)], send_sem.at[0])
    gone(z_out.at[pl.ds(0, NZ - 1), pl.ds(0, CODED)], send_sem.at[1])
    gone(stat_z.at[pl.ds(0, len(line)), pl.ds(0, 1)], send_sem.at[2])
    gone(stat_p.at[pl.ds(0, len(plane)), pl.ds(0, 2)], send_sem.at[3])

    for back in ARRIVALS:
        landed(weights.at[(z - back) % NZ, x], gr_sem.at[back])
        for o in RELAYS.get(back, ()):
            g_copy(back, o).start()
        spread(back)
        if back == 11:
            landed(weights.at[z, pl.ds(0, NX - 1)], land_sem.at[3])
            for o in NEAR:
                r_copy(o).start()
    landed(weights.at[pl.ds(0, len(ARRIVALS)), pl.ds(0, NX - 1)], land_sem.at[4])
    landed(weights.at[pl.ds(0, len(NEAR))], land_sem.at[5])

    gone(weights.at[pl.ds(0, len(ARRIVALS)), 0], send_sem.at[4])
    gone(weights.at[pl.ds(0, 1 + len(ARRIVALS)), pl.ds(0, NX - 1)], send_sem.at[5])
    gone(weights.at[pl.ds(0, len(NEAR))], send_sem.at[6])


def local(grads, piece_lengths, split_flags, master_params, exp_avg, exp_avg_sq):
    vmem = pl.BlockSpec(memory_space=pltpu.VMEM)
    anywhere = pl.BlockSpec(memory_space=pltpu.HBM)
    dma = pltpu.SemaphoreType.DMA
    hbm = lambda array: pltpu.with_memory_space_constraint(array, pltpu.HBM)
    made, model = pl.pallas_call(
        kernel,
        name="lamb",
        out_shape=(jax.ShapeDtypeStruct((3, ROWS, 128), jnp.float32), jax.ShapeDtypeStruct((NZ, NX, ROWS, 128), jnp.bfloat16)),
        in_specs=[anywhere] * 6,
        out_specs=(vmem, vmem),
        scratch_shapes=[
            pltpu.VMEM((NZ * NX * ROWS, 128), jnp.float32),
            pltpu.VMEM((NX, NZ, WORDS + 8, 128), jnp.int32),
            pltpu.VMEM((NX, NZ, WORDS + 8, 128), jnp.int32),
            pltpu.VMEM((NZ, WORDS + 8, 128), jnp.int32),
            pltpu.VMEM((NZ, WORDS + 8, 128), jnp.int32),
            pltpu.VMEM((ROWS, 128), jnp.float32),
            pltpu.VMEM((3, ROWS, 128), jnp.float32),
            pltpu.VMEM((NZ * 2, 8, 128), jnp.float32),
            pltpu.VMEM((NX * NY, 8, 128), jnp.float32),
            pltpu.SMEM((NP,), jnp.int32),
            pltpu.SMEM((NP,), jnp.int32),
            pltpu.SemaphoreType.REGULAR, dma((NZ,)), dma((3,)), dma((7,)), dma((6,)), dma((NZ,)), dma((NZ,)),
        ],
        compiler_params=pltpu.CompilerParams(
            collective_id=0, has_side_effects=True, vmem_limit_bytes=24 * 2**20
        ),
    )(
        hbm(piece_lengths), hbm(split_flags), hbm(grads.reshape(NZ * NX * ROWS, 128)),
        hbm(master_params.reshape(ROWS, 128)), hbm(exp_avg.reshape(ROWS, 128)), hbm(exp_avg_sq.reshape(ROWS, 128)),
    )
    model = lax.optimization_barrier(model.reshape(-1))
    return (
        made[0].reshape(1, -1), made[1].reshape(1, -1), made[2].reshape(1, -1), model.reshape(1, -1)
    )


def solution(mesh):
    return jax.shard_map(
        local,
        mesh=mesh,
        in_specs=(
            P("dp", "tensor", None),
            P(),
            P(),
            P("tensor", "dp"),
            P("tensor", "dp"),
            P("tensor", "dp"),
        ),
        out_specs=(P("tensor", "dp"), P("tensor", "dp"), P("tensor", "dp"), P("tensor", None)),
        check_vma=False,
    )
```

```python
import jax
import jax.numpy as jnp
from jax import lax
from jax.experimental import pallas as pl
from jax.experimental.pallas import tpu as pltpu
from jax.sharding import PartitionSpec as P

MESH = pl.DeviceIdType.MESH
NZ, NX, NY, NT = 16, 4, 4, 8
ROWS = 64
WORDS = 32
NP = 40
CODED = WORDS + 1


def encode(block, unit):
    top = jnp.max(jnp.abs(block), axis=0, keepdims=True)
    scale = (top * unit).astype(jnp.int32) + 1
    inverse = (32767.0 * unit) / scale.astype(jnp.float32)
    codes = jnp.round(block * inverse).astype(jnp.int32)
    return (codes[:WORDS] << 16) + codes[WORDS:], scale


def decode(words, scale, unit):
    step = scale.astype(jnp.float32) * (1.0 / (32767.0 * unit))
    high = ((words + 32768) >> 16).astype(jnp.float32) * step
    low = ((words << 16) >> 16).astype(jnp.float32) * step
    return high, low


NEAR = (2, 14, 1, 15)
LONG = (8, 5, 11, 3, 13)
RELAYS = {3: (1,), 13: (15,), 5: (2, 1), 11: (14, 15), 8: ()}
ARRIVALS = (3, 13, 5, 11, 4, 12, 8, 6, 10, 7, 9)
REDUCED = (8, 7, 9, 6, 10, 4, 12, 5, 11, 3, 13)
SENT = (8, 2, 14, 7, 1, 15, 9, 6, 10, 4, 12, 5, 11, 3, 13)
BY_WAY = {7: (2, 0), 6: (1, 1), 9: (14, 2), 10: (15, 3), 4: (1, 4), 12: (15, 5)}
MERGED = {5: (0, 2), 11: (2, 2), 3: (4, 1), 13: (5, 1)}
OWN_AT = 6
DIRECT = (8, 5, 11, 3, 13)
FAR_FIRST = (8, 7, 9, 6, 10, 5, 11, 4, 12, 3, 13, 2, 14, 1, 15)

UNIT_X = float(2**26)
UNIT_Z = float(2**23)


def piece_sums(values, position, starts, first):
    rows = []
    for k in range(NP):
        inside = (position >= starts[k]) & (position < starts[k + 1])
        rows.append(jnp.sum(jnp.where(inside, values, 0.0), axis=0, keepdims=True))
    table = jnp.concatenate(rows, axis=0)
    totals = jnp.sum(table, axis=1, keepdims=True)
    piece = lax.broadcasted_iota(jnp.int32, (NP, 128), 0)
    lane = lax.broadcasted_iota(jnp.int32, (NP, 128), 1)
    return jnp.sum(jnp.where(piece + first == lane, totals, 0.0), axis=0, keepdims=True)


def kernel(
    lengths_in, flags_in, grads, master, avg, avg_sq,
    made, weights,
    held, coded, row_in, x_in, z_out, way_in, z_in, total, state, stat_z, stat_p, lengths, flags,
    word_sem, load_sem, state_sem, send_sem, land_sem, xr_sem, way_sem, gr_sem,
):
    dp = lax.axis_index("dp")
    t = lax.axis_index("tensor")
    z, x = dp // NX, dp % NX

    def at(zz, xx, tt):
        return (zz * NX + xx, tt)

    def landed(ref, sem):
        pltpu.make_async_remote_copy(
            src_ref=ref, dst_ref=ref, send_sem=sem, recv_sem=sem,
            device_id=at(z, (x + 1) % NX, t), device_id_type=MESH,
        ).wait_recv()

    def gone(ref, sem):
        pltpu.make_async_remote_copy(
            src_ref=ref, dst_ref=ref, send_sem=sem, recv_sem=sem,
            device_id=at(z, (x + 1) % NX, t), device_id_type=MESH,
        ).wait_send()

    def load(zz):
        rows = pl.ds(pl.multiple_of(zz * (NX * ROWS), NX * ROWS), NX * ROWS)
        return pltpu.make_async_copy(grads.at[rows], held.at[rows], load_sem.at[zz])

    for o in (*SENT, 0):
        load((z + o) % NZ).start()
    for i, ref in enumerate((master, avg, avg_sq)):
        pltpu.make_async_copy(ref, state.at[i], state_sem.at[0]).start()
    tables = [
        pltpu.make_async_copy(lengths_in, lengths, state_sem.at[1]),
        pltpu.make_async_copy(flags_in, flags, state_sem.at[2]),
    ]
    for copy in tables:
        copy.start()

    barrier = pltpu.get_barrier_semaphore()

    y, core = t // 2, t % 2

    def near(dx, dy, dc):
        return at(z, (x + dx) % NX, ((y + dy) % NY) * 2 + (core + dc) % 2)

    greeted = [near(dx, 0, 0) for dx in range(1, NX)]
    greeted += [near(0, dy, dc) for dy in range(NY) for dc in range(2) if dy or dc]
    greeted += [at((z + o) % NZ, x, t) for o in (1, 15, 2, 14, 3, 13, 4, 12)]
    for device in greeted:
        pl.semaphore_signal(barrier, 1, device_id=device, device_id_type=MESH)

    def x_copy(zz, dx):
        xx = (x + dx) % NX
        return pltpu.make_async_remote_copy(
            src_ref=coded.at[xx, zz, pl.ds(0, CODED)], dst_ref=x_in.at[x, zz, pl.ds(0, CODED)],
            send_sem=send_sem.at[0], recv_sem=xr_sem.at[zz],
            device_id=at(z, xx, t), device_id_type=MESH,
        )

    pl.semaphore_wait(barrier, len(greeted))
    for o in (4, 12):
        pl.semaphore_signal(word_sem, 1, device_id=at((z + o) % NZ, x, t), device_id_type=MESH)

    def code(zz, xx):
        start = pl.multiple_of((zz * NX + xx) * ROWS, ROWS)
        words, scale = encode(held[pl.ds(start, ROWS), :], UNIT_X)
        coded[xx, zz, :WORDS, :] = words
        coded[xx, zz, WORDS:CODED, :] = scale

    for o in SENT:
        zz = (z + o) % NZ
        load(zz).wait()
        if o in NEAR:
            for xx in range(NX):
                code(zz, xx)
            pltpu.make_async_remote_copy(
                src_ref=coded.at[:, zz, pl.ds(0, CODED)],
                dst_ref=row_in.at[NEAR.index(o), :, pl.ds(0, CODED)],
                send_sem=send_sem.at[7], recv_sem=land_sem.at[6],
                device_id=at(zz, x, t), device_id_type=MESH,
            ).start()
        else:
            for dx in (2, 1, 3):
                code(zz, (x + dx) % NX)
                x_copy(zz, dx).start()

    for copy in tables:
        copy.wait()
    pltpu.make_async_copy(state, state, state_sem.at[0]).wait()
    starts = [jnp.int32(0)]
    split = jnp.zeros((1, 128), jnp.int32)
    lane = lax.broadcasted_iota(jnp.int32, (1, 128), 1)
    for k in range(NP):
        starts.append(starts[-1] + lengths[k])
        split = jnp.where((lane == k) | (lane == k + 64), flags[k], split)
    position = (
        dp * (ROWS * 128)
        + lax.broadcasted_iota(jnp.int32, (ROWS, 128), 0) * 128
        + lax.broadcasted_iota(jnp.int32, (ROWS, 128), 1)
    )
    w = state[0]
    w_sums = piece_sums(w * w, position, starts, 0)

    def sum_over_x(zz, high, low, unit):
        landed(x_in.at[pl.ds(0, NX - 1), zz, pl.ds(0, CODED)], xr_sem.at[zz])
        for dx in (1, 3, 2):
            xx = (x + dx) % NX
            h, l = decode(x_in[xx, zz, :WORDS, :], x_in[xx, zz, WORDS:CODED, :], unit)
            high, low = high + h, low + l
        return high, low

    def halves(zz, xx):
        start = pl.multiple_of((zz * NX + xx) * ROWS, ROWS)
        return held[pl.ds(start, WORDS), :], held[pl.ds(pl.multiple_of(start + WORDS, WORDS), WORDS), :]

    def sum_over_near(xx):
        high, low = halves(z, xx)
        for n in range(len(NEAR)):
            h, l = decode(row_in[n, xx, :WORDS, :], row_in[n, xx, WORDS:CODED, :], UNIT_X)
            high, low = high + h, low + l
        return high, low

    pl.semaphore_wait(word_sem, 2)
    for n, o in enumerate(REDUCED):
        if n == OWN_AT:
            load(z).wait()
            landed(row_in.at[:, :, pl.ds(0, CODED)], land_sem.at[6])
            for dx in (2, 1, 3):
                xx = (x + dx) % NX
                words, scale = encode(jnp.concatenate(sum_over_near(xx), axis=0), UNIT_Z)
                coded[xx, z, :WORDS, :] = words
                coded[xx, z, WORDS:CODED, :] = scale
                x_copy(z, dx).start()
            high, low = sum_over_near(x)
            total[:WORDS, :] = high
            total[WORDS:, :] = low
        zz = (z + o) % NZ
        high, low = sum_over_x(zz, *halves(zz, x), UNIT_X)
        if o in MERGED:
            first, count = MERGED[o]
            landed(way_in.at[pl.ds(first, count), pl.ds(0, CODED)], way_sem.at[first])
            for slot in range(first, first + count):
                h, l = decode(way_in[slot, :WORDS, :], way_in[slot, WORDS:CODED, :], UNIT_Z)
                high, low = high + h, low + l
        words, scale = encode(jnp.concatenate([high, low], axis=0), UNIT_Z)
        z_out[n, :WORDS, :] = words
        z_out[n, WORDS:CODED, :] = scale
        if o in BY_WAY:
            to, slot = BY_WAY[o]
            target, sem = way_in.at[slot], way_sem.at[0 if slot < 2 else 2 if slot < 4 else slot]
        else:
            to = o
            target, sem = z_in.at[DIRECT.index(o)], land_sem.at[0]
        pltpu.make_async_remote_copy(
            src_ref=z_out.at[n, pl.ds(0, CODED)], dst_ref=target.at[pl.ds(0, CODED)],
            send_sem=send_sem.at[1], recv_sem=sem,
            device_id=at((z + to) % NZ, x, t), device_id_type=MESH,
        ).start()
    high, low = sum_over_x(z, total[:WORDS, :], total[WORDS:, :], UNIT_Z)
    landed(z_in.at[pl.ds(0, len(DIRECT)), pl.ds(0, CODED)], land_sem.at[0])
    for n in range(len(DIRECT)):
        h, l = decode(z_in[n, :WORDS, :], z_in[n, WORDS:CODED, :], UNIT_Z)
        high, low = high + h, low + l
    total[:WORDS, :] = high
    total[WORDS:, :] = low

    grad = total[...] * (1.0 / (NZ * NX))
    new_avg = 0.9 * state[1] + 0.1 * grad
    new_avg_sq = 0.95 * state[2] + 0.05 * grad * grad
    made[1] = new_avg
    made[2] = new_avg_sq
    update = new_avg / (jnp.sqrt(new_avg_sq) + 1e-08) + 0.1 * state[0]
    total[...] = update
    u_sums = piece_sums(update * update, position, starts, 64)

    mine = z * 2 + core
    stat_z[mine, 0:1, :] = w_sums + u_sums
    line = [(o, dc) for o in FAR_FIRST for dc in (1, 0)] + [(0, 1)]
    for o, dc in line:
        pltpu.make_async_remote_copy(
            src_ref=stat_z.at[mine, pl.ds(0, 1)], dst_ref=stat_z.at[mine, pl.ds(0, 1)],
            send_sem=send_sem.at[2], recv_sem=land_sem.at[1],
            device_id=at((z + o) % NZ, x, y * 2 + (core + dc) % 2), device_id_type=MESH,
        ).start()
    landed(stat_z.at[pl.ds(0, len(line)), pl.ds(0, 1)], land_sem.at[1])
    own = stat_z[core, 0:1, :]
    other = stat_z[1 - core, 0:1, :]
    for zz in range(1, NZ):
        own = own + stat_z[zz * 2 + core, 0:1, :]
        other = other + stat_z[zz * 2 + 1 - core, 0:1, :]
    me = x * NY + y
    stat_p[me, 0:1, :] = own
    stat_p[me, 1:2, :] = own + other
    plane = [(dx, dy) for dx in (2, 1, 3, 0) for dy in (2, 1, 3, 0) if dx or dy]
    for dx, dy in plane:
        pltpu.make_async_remote_copy(
            src_ref=stat_p.at[me, pl.ds(0, 2)], dst_ref=stat_p.at[me, pl.ds(0, 2)],
            send_sem=send_sem.at[3], recv_sem=land_sem.at[2],
            device_id=near(dx, dy, 0), device_id_type=MESH,
        ).start()
    landed(stat_p.at[pl.ds(0, len(plane)), pl.ds(0, 2)], land_sem.at[2])
    data_sum = stat_p[y, 0:1, :]
    for xx in range(1, NX):
        data_sum = data_sum + stat_p[xx * NY + y, 0:1, :]
    tensor_sum = stat_p[0, 1:2, :]
    for i in range(1, NX * NY):
        tensor_sum = tensor_sum + stat_p[i, 1:2, :]
    effective = jnp.where(split == 1, tensor_sum, data_sum)
    norms = jnp.sqrt(effective)
    trust = norms / jnp.maximum(pltpu.roll(norms, 64, 1), 1.0)
    trust_at = jnp.broadcast_to(trust[:, 0:1], (ROWS, 128))
    for k in range(1, NP):
        trust_at = jnp.where(position >= starts[k], trust[:, k : k + 1], trust_at)
    new_weights = state[0] - 0.05 * trust_at * total[...]

    weights[z, x] = new_weights.astype(jnp.bfloat16)

    def g_copy(back, o):
        block = weights.at[(z - back) % NZ, x]
        return pltpu.make_async_remote_copy(
            src_ref=block, dst_ref=block,
            send_sem=send_sem.at[4], recv_sem=gr_sem.at[(back + o) % NZ],
            device_id=at((z + o) % NZ, x, t), device_id_type=MESH,
        )

    def f_copy(back, dx):
        block = weights.at[(z - back) % NZ, x]
        return pltpu.make_async_remote_copy(
            src_ref=block, dst_ref=block,
            send_sem=send_sem.at[5], recv_sem=land_sem.at[4 if back else 3],
            device_id=at(z, (x + dx) % NX, t), device_id_type=MESH,
        )

    def r_copy(o):
        return pltpu.make_async_remote_copy(
            src_ref=weights.at[z], dst_ref=weights.at[z],
            send_sem=send_sem.at[6], recv_sem=land_sem.at[5],
            device_id=at((z + o) % NZ, x, t), device_id_type=MESH,
        )

    def spread(back):
        for dx in (2, 1, 3):
            f_copy(back, dx).start()

    for o in LONG:
        g_copy(0, o).start()
    spread(0)
    made[0] = new_weights

    gone(coded.at[pl.ds(0, NX - 1), pl.ds(0, len(REDUCED) + 1), pl.ds(0, CODED)], send_sem.at[0])
    gone(coded.at[:, pl.ds(0, len(NEAR)), pl.ds(0, CODED)], send_sem.at[7])
    gone(z_out.at[pl.ds(0, len(REDUCED)), pl.ds(0, CODED)], send_sem.at[1])
    gone(stat_z.at[pl.ds(0, len(line)), pl.ds(0, 1)], send_sem.at[2])
    gone(stat_p.at[pl.ds(0, len(plane)), pl.ds(0, 2)], send_sem.at[3])

    for back in ARRIVALS:
        landed(weights.at[(z - back) % NZ, x], gr_sem.at[back])
        for o in RELAYS.get(back, ()):
            g_copy(back, o).start()
        spread(back)
        if back == 11:
            landed(weights.at[z, pl.ds(0, NX - 1)], land_sem.at[3])
            for o in NEAR:
                r_copy(o).start()
    landed(weights.at[pl.ds(0, len(ARRIVALS)), pl.ds(0, NX - 1)], land_sem.at[4])
    landed(weights.at[pl.ds(0, len(NEAR))], land_sem.at[5])

    gone(weights.at[pl.ds(0, len(ARRIVALS)), 0], send_sem.at[4])
    gone(weights.at[pl.ds(0, 1 + len(ARRIVALS)), pl.ds(0, NX - 1)], send_sem.at[5])
    gone(weights.at[pl.ds(0, len(NEAR))], send_sem.at[6])


def local(grads, piece_lengths, split_flags, master_params, exp_avg, exp_avg_sq):
    vmem = pl.BlockSpec(memory_space=pltpu.VMEM)
    anywhere = pl.BlockSpec(memory_space=pltpu.HBM)
    dma = pltpu.SemaphoreType.DMA
    hbm = lambda array: pltpu.with_memory_space_constraint(array, pltpu.HBM)
    made, model = pl.pallas_call(
        kernel,
        name="lamb",
        out_shape=(jax.ShapeDtypeStruct((3, ROWS, 128), jnp.float32), jax.ShapeDtypeStruct((NZ, NX, ROWS, 128), jnp.bfloat16)),
        in_specs=[anywhere] * 6,
        out_specs=(vmem, vmem),
        scratch_shapes=[
            pltpu.VMEM((NZ * NX * ROWS, 128), jnp.float32),
            pltpu.VMEM((NX, NZ, WORDS + 8, 128), jnp.int32),
            pltpu.VMEM((len(NEAR), NX, WORDS + 8, 128), jnp.int32),
            pltpu.VMEM((NX, NZ, WORDS + 8, 128), jnp.int32),
            pltpu.VMEM((NZ, WORDS + 8, 128), jnp.int32),
            pltpu.VMEM((len(BY_WAY), WORDS + 8, 128), jnp.int32),
            pltpu.VMEM((len(DIRECT), WORDS + 8, 128), jnp.int32),
            pltpu.VMEM((ROWS, 128), jnp.float32),
            pltpu.VMEM((3, ROWS, 128), jnp.float32),
            pltpu.VMEM((NZ * 2, 8, 128), jnp.float32),
            pltpu.VMEM((NX * NY, 8, 128), jnp.float32),
            pltpu.SMEM((NP,), jnp.int32),
            pltpu.SMEM((NP,), jnp.int32),
            pltpu.SemaphoreType.REGULAR, dma((NZ,)), dma((3,)), dma((8,)), dma((7,)), dma((NZ,)), dma((6,)), dma((NZ,)),
        ],
        compiler_params=pltpu.CompilerParams(
            collective_id=0, has_side_effects=True, vmem_limit_bytes=24 * 2**20
        ),
    )(
        hbm(piece_lengths), hbm(split_flags), hbm(grads.reshape(NZ * NX * ROWS, 128)),
        hbm(master_params.reshape(ROWS, 128)), hbm(exp_avg.reshape(ROWS, 128)), hbm(exp_avg_sq.reshape(ROWS, 128)),
    )
    model = lax.optimization_barrier(model.reshape(-1))
    return (
        made[0].reshape(1, -1), made[1].reshape(1, -1), made[2].reshape(1, -1), model.reshape(1, -1)
    )


def solution(mesh):
    return jax.shard_map(
        local,
        mesh=mesh,
        in_specs=(
            P("dp", "tensor", None),
            P(),
            P(),
            P("tensor", "dp"),
            P("tensor", "dp"),
            P("tensor", "dp"),
        ),
        out_specs=(P("tensor", "dp"), P("tensor", "dp"), P("tensor", "dp"), P("tensor", None)),
        check_vma=False,
    )
```

```python
import jax
import jax.numpy as jnp
from jax import lax
from jax.experimental import pallas as pl
from jax.experimental.pallas import tpu as pltpu
from jax.sharding import PartitionSpec as P

MESH = pl.DeviceIdType.MESH
NZ, NX, NY, NT = 16, 4, 4, 8
ROWS = 64
WORDS = 32
NP = 40
CODED = WORDS + 1


def encode(block, unit):
    top = jnp.max(jnp.abs(block), axis=0, keepdims=True)
    scale = (top * unit).astype(jnp.int32) + 1
    inverse = (32767.0 * unit) / scale.astype(jnp.float32)
    codes = jnp.round(block * inverse).astype(jnp.int32)
    return (codes[:WORDS] << 16) + codes[WORDS:], scale


def decode(words, scale, unit):
    step = scale.astype(jnp.float32) * (1.0 / (32767.0 * unit))
    high = ((words + 32768) >> 16).astype(jnp.float32) * step
    low = ((words << 16) >> 16).astype(jnp.float32) * step
    return high, low


NEAR = (2, 14, 1, 15)
LONG = (8, 5, 11, 3, 13)
RELAYS = {3: (1,), 13: (15,), 5: (2, 1), 11: (14, 15), 8: ()}
ARRIVALS = (3, 13, 5, 11, 4, 12, 8, 6, 10, 7, 9)
REDUCED = (8, 7, 9, 6, 10, 4, 12, 5, 11, 3, 13)
SENT = (8, 2, 14, 7, 1, 15, 9, 6, 10, 4, 12, 5, 11, 3, 13)
BY_WAY = {7: (2, 0), 6: (1, 1), 9: (14, 2), 10: (15, 3), 4: (1, 4), 12: (15, 5)}
MERGED = {5: (0, 2), 11: (2, 2), 3: (4, 1), 13: (5, 1)}
OWN_AT = 6
DIRECT = (8, 5, 11, 3, 13)
FAR_FIRST = (8, 7, 9, 6, 10, 5, 11, 4, 12, 3, 13, 2, 14, 1, 15)

UNIT_X = float(2**26)
UNIT_Z = float(2**23)


def piece_sums(values, position, starts, first):
    rows = []
    for k in range(NP):
        inside = (position >= starts[k]) & (position < starts[k + 1])
        rows.append(jnp.sum(jnp.where(inside, values, 0.0), axis=0, keepdims=True))
    table = jnp.concatenate(rows, axis=0)
    totals = jnp.sum(table, axis=1, keepdims=True)
    piece = lax.broadcasted_iota(jnp.int32, (NP, 128), 0)
    lane = lax.broadcasted_iota(jnp.int32, (NP, 128), 1)
    return jnp.sum(jnp.where(piece + first == lane, totals, 0.0), axis=0, keepdims=True)


def kernel(
    lengths_in, flags_in, grads, master, avg, avg_sq,
    made, model,
    weights, held, coded, row_in, x_in, z_out, way_in, z_in, total, state, stat_z, stat_p, lengths, flags,
    word_sem, load_sem, state_sem, send_sem, land_sem, xr_sem, way_sem, gr_sem,
):
    dp = lax.axis_index("dp")
    t = lax.axis_index("tensor")
    z, x = dp // NX, dp % NX

    def at(zz, xx, tt):
        return (zz * NX + xx, tt)

    def landed(ref, sem):
        pltpu.make_async_remote_copy(
            src_ref=ref, dst_ref=ref, send_sem=sem, recv_sem=sem,
            device_id=at(z, (x + 1) % NX, t), device_id_type=MESH,
        ).wait_recv()

    def gone(ref, sem):
        pltpu.make_async_remote_copy(
            src_ref=ref, dst_ref=ref, send_sem=sem, recv_sem=sem,
            device_id=at(z, (x + 1) % NX, t), device_id_type=MESH,
        ).wait_send()

    def load(zz):
        rows = pl.ds(pl.multiple_of(zz * (NX * ROWS), NX * ROWS), NX * ROWS)
        return pltpu.make_async_copy(grads.at[rows], held.at[rows], load_sem.at[zz])

    for o in (*SENT, 0):
        load((z + o) % NZ).start()
    for i, ref in enumerate((master, avg, avg_sq)):
        pltpu.make_async_copy(ref, state.at[i], state_sem.at[0]).start()
    tables = [
        pltpu.make_async_copy(lengths_in, lengths, state_sem.at[1]),
        pltpu.make_async_copy(flags_in, flags, state_sem.at[2]),
    ]
    for copy in tables:
        copy.start()

    barrier = pltpu.get_barrier_semaphore()

    y, core = t // 2, t % 2

    def near(dx, dy, dc):
        return at(z, (x + dx) % NX, ((y + dy) % NY) * 2 + (core + dc) % 2)

    greeted = [near(dx, 0, 0) for dx in range(1, NX)]
    greeted += [near(0, dy, dc) for dy in range(NY) for dc in range(2) if dy or dc]
    greeted += [at((z + o) % NZ, x, t) for o in (1, 15, 2, 14, 3, 13, 4, 12)]
    for device in greeted:
        pl.semaphore_signal(barrier, 1, device_id=device, device_id_type=MESH)

    def x_copy(zz, dx):
        xx = (x + dx) % NX
        return pltpu.make_async_remote_copy(
            src_ref=coded.at[xx, zz, pl.ds(0, CODED)], dst_ref=x_in.at[x, zz, pl.ds(0, CODED)],
            send_sem=send_sem.at[0], recv_sem=xr_sem.at[zz],
            device_id=at(z, xx, t), device_id_type=MESH,
        )

    pl.semaphore_wait(barrier, len(greeted))
    for o in (4, 12):
        pl.semaphore_signal(word_sem, 1, device_id=at((z + o) % NZ, x, t), device_id_type=MESH)

    def code(zz, xx):
        start = pl.multiple_of((zz * NX + xx) * ROWS, ROWS)
        words, scale = encode(held[pl.ds(start, ROWS), :], UNIT_X)
        coded[xx, zz, :WORDS, :] = words
        coded[xx, zz, WORDS:CODED, :] = scale

    for o in SENT:
        zz = (z + o) % NZ
        load(zz).wait()
        if o in NEAR:
            for xx in range(NX):
                code(zz, xx)
            pltpu.make_async_remote_copy(
                src_ref=coded.at[:, zz, pl.ds(0, CODED)],
                dst_ref=row_in.at[NEAR.index(o), :, pl.ds(0, CODED)],
                send_sem=send_sem.at[7], recv_sem=land_sem.at[6],
                device_id=at(zz, x, t), device_id_type=MESH,
            ).start()
        else:
            for dx in (2, 1, 3):
                code(zz, (x + dx) % NX)
                x_copy(zz, dx).start()

    for copy in tables:
        copy.wait()
    pltpu.make_async_copy(state, state, state_sem.at[0]).wait()
    starts = [jnp.int32(0)]
    split = jnp.zeros((1, 128), jnp.int32)
    lane = lax.broadcasted_iota(jnp.int32, (1, 128), 1)
    for k in range(NP):
        starts.append(starts[-1] + lengths[k])
        split = jnp.where((lane == k) | (lane == k + 64), flags[k], split)
    position = (
        dp * (ROWS * 128)
        + lax.broadcasted_iota(jnp.int32, (ROWS, 128), 0) * 128
        + lax.broadcasted_iota(jnp.int32, (ROWS, 128), 1)
    )
    w = state[0]
    w_sums = piece_sums(w * w, position, starts, 0)

    def sum_over_x(zz, high, low, unit):
        landed(x_in.at[pl.ds(0, NX - 1), zz, pl.ds(0, CODED)], xr_sem.at[zz])
        for dx in (1, 3, 2):
            xx = (x + dx) % NX
            h, l = decode(x_in[xx, zz, :WORDS, :], x_in[xx, zz, WORDS:CODED, :], unit)
            high, low = high + h, low + l
        return high, low

    def halves(zz, xx):
        start = pl.multiple_of((zz * NX + xx) * ROWS, ROWS)
        return held[pl.ds(start, WORDS), :], held[pl.ds(pl.multiple_of(start + WORDS, WORDS), WORDS), :]

    def sum_over_near(xx):
        high, low = halves(z, xx)
        for n in range(len(NEAR)):
            h, l = decode(row_in[n, xx, :WORDS, :], row_in[n, xx, WORDS:CODED, :], UNIT_X)
            high, low = high + h, low + l
        return high, low

    pl.semaphore_wait(word_sem, 2)
    for n, o in enumerate(REDUCED):
        if n == OWN_AT:
            load(z).wait()
            landed(row_in.at[:, :, pl.ds(0, CODED)], land_sem.at[6])
            for dx in (2, 1, 3):
                xx = (x + dx) % NX
                words, scale = encode(jnp.concatenate(sum_over_near(xx), axis=0), UNIT_Z)
                coded[xx, z, :WORDS, :] = words
                coded[xx, z, WORDS:CODED, :] = scale
                x_copy(z, dx).start()
            high, low = sum_over_near(x)
            total[:WORDS, :] = high
            total[WORDS:, :] = low
        zz = (z + o) % NZ
        high, low = sum_over_x(zz, *halves(zz, x), UNIT_X)
        if o in MERGED:
            first, count = MERGED[o]
            landed(way_in.at[pl.ds(first, count), pl.ds(0, CODED)], way_sem.at[first])
            for slot in range(first, first + count):
                h, l = decode(way_in[slot, :WORDS, :], way_in[slot, WORDS:CODED, :], UNIT_Z)
                high, low = high + h, low + l
        words, scale = encode(jnp.concatenate([high, low], axis=0), UNIT_Z)
        z_out[n, :WORDS, :] = words
        z_out[n, WORDS:CODED, :] = scale
        if o in BY_WAY:
            to, slot = BY_WAY[o]
            target, sem = way_in.at[slot], way_sem.at[0 if slot < 2 else 2 if slot < 4 else slot]
        else:
            to = o
            target, sem = z_in.at[DIRECT.index(o)], land_sem.at[0]
        pltpu.make_async_remote_copy(
            src_ref=z_out.at[n, pl.ds(0, CODED)], dst_ref=target.at[pl.ds(0, CODED)],
            send_sem=send_sem.at[1], recv_sem=sem,
            device_id=at((z + to) % NZ, x, t), device_id_type=MESH,
        ).start()
    high, low = sum_over_x(z, total[:WORDS, :], total[WORDS:, :], UNIT_Z)
    landed(z_in.at[pl.ds(0, len(DIRECT)), pl.ds(0, CODED)], land_sem.at[0])
    for n in range(len(DIRECT)):
        h, l = decode(z_in[n, :WORDS, :], z_in[n, WORDS:CODED, :], UNIT_Z)
        high, low = high + h, low + l
    total[:WORDS, :] = high
    total[WORDS:, :] = low

    grad = total[...] * (1.0 / (NZ * NX))
    new_avg = 0.9 * state[1] + 0.1 * grad
    new_avg_sq = 0.95 * state[2] + 0.05 * grad * grad
    made[1] = new_avg
    made[2] = new_avg_sq
    update = new_avg / (jnp.sqrt(new_avg_sq) + 1e-08) + 0.1 * state[0]
    total[...] = update
    u_sums = piece_sums(update * update, position, starts, 64)

    mine = z * 2 + core
    stat_z[mine, 0:1, :] = w_sums + u_sums
    line = [(o, dc) for o in FAR_FIRST for dc in (1, 0)] + [(0, 1)]
    for o, dc in line:
        pltpu.make_async_remote_copy(
            src_ref=stat_z.at[mine, pl.ds(0, 1)], dst_ref=stat_z.at[mine, pl.ds(0, 1)],
            send_sem=send_sem.at[2], recv_sem=land_sem.at[1],
            device_id=at((z + o) % NZ, x, y * 2 + (core + dc) % 2), device_id_type=MESH,
        ).start()
    landed(stat_z.at[pl.ds(0, len(line)), pl.ds(0, 1)], land_sem.at[1])
    own = stat_z[core, 0:1, :]
    other = stat_z[1 - core, 0:1, :]
    for zz in range(1, NZ):
        own = own + stat_z[zz * 2 + core, 0:1, :]
        other = other + stat_z[zz * 2 + 1 - core, 0:1, :]
    me = x * NY + y
    stat_p[me, 0:1, :] = own
    stat_p[me, 1:2, :] = own + other
    plane = [(dx, dy) for dx in (2, 1, 3, 0) for dy in (2, 1, 3, 0) if dx or dy]
    for dx, dy in plane:
        pltpu.make_async_remote_copy(
            src_ref=stat_p.at[me, pl.ds(0, 2)], dst_ref=stat_p.at[me, pl.ds(0, 2)],
            send_sem=send_sem.at[3], recv_sem=land_sem.at[2],
            device_id=near(dx, dy, 0), device_id_type=MESH,
        ).start()
    landed(stat_p.at[pl.ds(0, len(plane)), pl.ds(0, 2)], land_sem.at[2])
    data_sum = stat_p[y, 0:1, :]
    for xx in range(1, NX):
        data_sum = data_sum + stat_p[xx * NY + y, 0:1, :]
    tensor_sum = stat_p[0, 1:2, :]
    for i in range(1, NX * NY):
        tensor_sum = tensor_sum + stat_p[i, 1:2, :]
    effective = jnp.where(split == 1, tensor_sum, data_sum)
    norms = jnp.sqrt(effective)
    trust = norms / jnp.maximum(pltpu.roll(norms, 64, 1), 1.0)
    trust_at = jnp.broadcast_to(trust[:, 0:1], (ROWS, 128))
    for k in range(1, NP):
        trust_at = jnp.where(position >= starts[k], trust[:, k : k + 1], trust_at)
    new_weights = state[0] - 0.05 * trust_at * total[...]

    weights[z, x] = new_weights.astype(jnp.bfloat16)

    def g_copy(back, o):
        block = weights.at[(z - back) % NZ, x]
        return pltpu.make_async_remote_copy(
            src_ref=block, dst_ref=block,
            send_sem=send_sem.at[4], recv_sem=gr_sem.at[(back + o) % NZ],
            device_id=at((z + o) % NZ, x, t), device_id_type=MESH,
        )

    def f_copy(back, dx):
        block = weights.at[(z - back) % NZ, x]
        return pltpu.make_async_remote_copy(
            src_ref=block, dst_ref=block,
            send_sem=send_sem.at[5], recv_sem=xr_sem.at[back],
            device_id=at(z, (x + dx) % NX, t), device_id_type=MESH,
        )

    def r_copy(o):
        return pltpu.make_async_remote_copy(
            src_ref=weights.at[z], dst_ref=weights.at[z],
            send_sem=send_sem.at[6], recv_sem=way_sem.at[NEAR.index(o)],
            device_id=at((z + o) % NZ, x, t), device_id_type=MESH,
        )

    def spread(back):
        for dx in (2, 1, 3):
            f_copy(back, dx).start()

    for o in LONG:
        g_copy(0, o).start()
    spread(0)
    made[0] = new_weights

    gone(coded.at[pl.ds(0, NX - 1), pl.ds(0, len(REDUCED) + 1), pl.ds(0, CODED)], send_sem.at[0])
    gone(coded.at[:, pl.ds(0, len(NEAR)), pl.ds(0, CODED)], send_sem.at[7])
    gone(z_out.at[pl.ds(0, len(REDUCED)), pl.ds(0, CODED)], send_sem.at[1])
    gone(stat_z.at[pl.ds(0, len(line)), pl.ds(0, 1)], send_sem.at[2])
    gone(stat_p.at[pl.ds(0, len(plane)), pl.ds(0, 2)], send_sem.at[3])

    for back in ARRIVALS:
        landed(weights.at[(z - back) % NZ, x], gr_sem.at[back])
        for o in RELAYS.get(back, ()):
            g_copy(back, o).start()
        spread(back)
        if back == 11:
            landed(weights.at[z, pl.ds(0, NX - 1)], xr_sem.at[0])
            for o in NEAR:
                r_copy(o).start()

    for back in (0, 3, 13, 5, 11, 1, 15, 4, 12, 2, 14, 8, 6, 10, 7, 9):
        zz = (z - back) % NZ
        if back in NEAR:
            landed(weights.at[zz], way_sem.at[NEAR.index(back)])
        elif back:
            landed(weights.at[zz, pl.ds(0, NX - 1)], xr_sem.at[back])

        def place(xx, c, zz=zz):
            start = pl.multiple_of((zz * NX + xx) * ROWS, ROWS)
            model[pl.ds(start, ROWS), :, :] = weights[zz, xx][:, None, :]
            return c

        lax.fori_loop(0, NX, place, 0)

    gone(weights.at[pl.ds(0, len(ARRIVALS)), 0], send_sem.at[4])
    gone(weights.at[pl.ds(0, 1 + len(ARRIVALS)), pl.ds(0, NX - 1)], send_sem.at[5])
    gone(weights.at[pl.ds(0, len(NEAR))], send_sem.at[6])


def local(grads, piece_lengths, split_flags, master_params, exp_avg, exp_avg_sq):
    vmem = pl.BlockSpec(memory_space=pltpu.VMEM)
    anywhere = pl.BlockSpec(memory_space=pltpu.HBM)
    dma = pltpu.SemaphoreType.DMA
    hbm = lambda array: pltpu.with_memory_space_constraint(array, pltpu.HBM)
    made, model = pl.pallas_call(
        kernel,
        name="lamb",
        out_shape=(jax.ShapeDtypeStruct((3, ROWS, 128), jnp.float32), jax.ShapeDtypeStruct((NZ * NX * ROWS, 1, 128), jnp.bfloat16)),
        in_specs=[anywhere] * 6,
        out_specs=(vmem, vmem),
        scratch_shapes=[
            pltpu.VMEM((NZ, NX, ROWS, 128), jnp.bfloat16),
            pltpu.VMEM((NZ * NX * ROWS, 128), jnp.float32),
            pltpu.VMEM((NX, NZ, WORDS + 8, 128), jnp.int32),
            pltpu.VMEM((len(NEAR), NX, WORDS + 8, 128), jnp.int32),
            pltpu.VMEM((NX, NZ, WORDS + 8, 128), jnp.int32),
            pltpu.VMEM((NZ, WORDS + 8, 128), jnp.int32),
            pltpu.VMEM((len(BY_WAY), WORDS + 8, 128), jnp.int32),
            pltpu.VMEM((len(DIRECT), WORDS + 8, 128), jnp.int32),
            pltpu.VMEM((ROWS, 128), jnp.float32),
            pltpu.VMEM((3, ROWS, 128), jnp.float32),
            pltpu.VMEM((NZ * 2, 8, 128), jnp.float32),
            pltpu.VMEM((NX * NY, 8, 128), jnp.float32),
            pltpu.SMEM((NP,), jnp.int32),
            pltpu.SMEM((NP,), jnp.int32),
            pltpu.SemaphoreType.REGULAR, dma((NZ,)), dma((3,)), dma((8,)), dma((7,)), dma((NZ,)), dma((6,)), dma((NZ,)),
        ],
        compiler_params=pltpu.CompilerParams(
            collective_id=0, has_side_effects=True, vmem_limit_bytes=24 * 2**20
        ),
    )(
        hbm(piece_lengths), hbm(split_flags), hbm(grads.reshape(NZ * NX * ROWS, 128)),
        hbm(master_params.reshape(ROWS, 128)), hbm(exp_avg.reshape(ROWS, 128)), hbm(exp_avg_sq.reshape(ROWS, 128)),
    )
    return (
        made[0].reshape(1, -1), made[1].reshape(1, -1), made[2].reshape(1, -1), model.reshape(1, -1)
    )


def solution(mesh):
    return jax.shard_map(
        local,
        mesh=mesh,
        in_specs=(
            P("dp", "tensor", None),
            P(),
            P(),
            P("tensor", "dp"),
            P("tensor", "dp"),
            P("tensor", "dp"),
        ),
        out_specs=(P("tensor", "dp"), P("tensor", "dp"), P("tensor", "dp"), P("tensor", None)),
        check_vma=False,
    )
```

```python
import jax
import jax.numpy as jnp
from jax import lax
from jax.experimental import pallas as pl
from jax.experimental.pallas import tpu as pltpu
from jax.sharding import PartitionSpec as P

MESH = pl.DeviceIdType.MESH
NZ, NX, NY, NT = 16, 4, 4, 8
ROWS = 64
WORDS = 32
NP = 40
CODED = WORDS + 1


def encode(block, unit):
    top = jnp.max(jnp.abs(block), axis=0, keepdims=True)
    scale = (top * unit).astype(jnp.int32) + 1
    inverse = (32767.0 * unit) / scale.astype(jnp.float32)
    codes = jnp.round(block * inverse).astype(jnp.int32)
    return (codes[:WORDS] << 16) + codes[WORDS:], scale


def decode(words, scale, unit):
    step = scale.astype(jnp.float32) * (1.0 / (32767.0 * unit))
    high = ((words + 32768) >> 16).astype(jnp.float32) * step
    low = ((words << 16) >> 16).astype(jnp.float32) * step
    return high, low


NEAR = (2, 14, 1, 15)
LONG = (8, 5, 11, 3, 13)
RELAYS = {3: (1,), 13: (15,), 5: (2, 1), 11: (14, 15), 8: ()}
ARRIVALS = (3, 13, 5, 11, 4, 12, 8, 6, 10, 7, 9)
REDUCED = (8, 7, 9, 6, 10, 4, 12, 5, 11, 3, 13)
SENT = (8, 2, 14, 7, 1, 15, 9, 6, 10, 4, 12, 5, 11, 3, 13)
BY_WAY = {7: (2, 0), 6: (1, 1), 9: (14, 2), 10: (15, 3), 4: (1, 4), 12: (15, 5)}
MERGED = {5: (0, 2), 11: (2, 2), 3: (4, 1), 13: (5, 1)}
OWN_AT = 6
DIRECT = (8, 5, 11, 3, 13)
FAR_FIRST = (8, 7, 9, 6, 10, 5, 11, 4, 12, 3, 13, 2, 14, 1, 15)

UNIT_X = float(2**26)
UNIT_Z = float(2**23)


def piece_sums(values, position, starts, first):
    rows = []
    for k in range(NP):
        inside = (position >= starts[k]) & (position < starts[k + 1])
        rows.append(jnp.sum(jnp.where(inside, values, 0.0), axis=0, keepdims=True))
    table = jnp.concatenate(rows, axis=0)
    totals = jnp.sum(table, axis=1, keepdims=True)
    piece = lax.broadcasted_iota(jnp.int32, (NP, 128), 0)
    lane = lax.broadcasted_iota(jnp.int32, (NP, 128), 1)
    return jnp.sum(jnp.where(piece + first == lane, totals, 0.0), axis=0, keepdims=True)


def kernel(
    lengths_in, flags_in, grads, master, avg, avg_sq,
    made, model,
    weights, held, coded, row_in, x_in, z_out, way_in, z_in, total, state, stat_z, stat_p, lengths, flags,
    word_sem, load_sem, state_sem, send_sem, land_sem, xr_sem, way_sem,
):
    dp = lax.axis_index("dp")
    t = lax.axis_index("tensor")
    z, x = dp // NX, dp % NX

    def at(zz, xx, tt):
        return (zz * NX + xx, tt)

    def landed(ref, sem):
        pltpu.make_async_remote_copy(
            src_ref=ref, dst_ref=ref, send_sem=sem, recv_sem=sem,
            device_id=at(z, (x + 1) % NX, t), device_id_type=MESH,
        ).wait_recv()

    def gone(ref, sem):
        pltpu.make_async_remote_copy(
            src_ref=ref, dst_ref=ref, send_sem=sem, recv_sem=sem,
            device_id=at(z, (x + 1) % NX, t), device_id_type=MESH,
        ).wait_send()

    barrier = pltpu.get_barrier_semaphore()

    y, core = t // 2, t % 2

    def near(dx, dy, dc):
        return at(z, (x + dx) % NX, ((y + dy) % NY) * 2 + (core + dc) % 2)

    greeted = [at((z + o) % NZ, x, t) for o in (4, 12, 3, 13, 2, 14, 1, 15)]
    greeted += [near(dx, 0, 0) for dx in range(1, NX)]
    greeted += [near(0, dy, dc) for dy in range(NY) for dc in range(2) if dy or dc]
    for device in greeted:
        pl.semaphore_signal(barrier, 1, device_id=device, device_id_type=MESH)

    def load(zz):
        rows = pl.ds(pl.multiple_of(zz * (NX * ROWS), NX * ROWS), NX * ROWS)
        return pltpu.make_async_copy(grads.at[rows], held.at[rows], load_sem.at[zz])

    for o in (*SENT, 0):
        load((z + o) % NZ).start()

    def x_copy(zz, dx):
        xx = (x + dx) % NX
        return pltpu.make_async_remote_copy(
            src_ref=coded.at[xx, zz, pl.ds(0, CODED)], dst_ref=x_in.at[x, zz, pl.ds(0, CODED)],
            send_sem=send_sem.at[0], recv_sem=xr_sem.at[zz],
            device_id=at(z, xx, t), device_id_type=MESH,
        )

    pl.semaphore_wait(barrier, len(greeted))
    for o in (4, 12):
        pl.semaphore_signal(word_sem, 1, device_id=at((z + o) % NZ, x, t), device_id_type=MESH)

    def code(zz, xx):
        start = pl.multiple_of((zz * NX + xx) * ROWS, ROWS)
        words, scale = encode(held[pl.ds(start, ROWS), :], UNIT_X)
        coded[xx, zz, :WORDS, :] = words
        coded[xx, zz, WORDS:CODED, :] = scale

    tables = [
        pltpu.make_async_copy(lengths_in, lengths, state_sem.at[1]),
        pltpu.make_async_copy(flags_in, flags, state_sem.at[2]),
    ]
    for n, o in enumerate(SENT):
        if n == 3:
            for i, ref in enumerate((master, avg, avg_sq)):
                pltpu.make_async_copy(ref, state.at[i], state_sem.at[0]).start()
            for copy in tables:
                copy.start()
        zz = (z + o) % NZ
        load(zz).wait()
        if o in NEAR:
            for xx in range(NX):
                code(zz, xx)
            pltpu.make_async_remote_copy(
                src_ref=coded.at[:, zz, pl.ds(0, CODED)],
                dst_ref=row_in.at[NEAR.index(o), :, pl.ds(0, CODED)],
                send_sem=send_sem.at[7], recv_sem=land_sem.at[3],
                device_id=at(zz, x, t), device_id_type=MESH,
            ).start()
        else:
            for dx in (2, 1, 3):
                code(zz, (x + dx) % NX)
                x_copy(zz, dx).start()

    for copy in tables:
        copy.wait()
    pltpu.make_async_copy(state, state, state_sem.at[0]).wait()
    starts = [jnp.int32(0)]
    split = jnp.zeros((1, 128), jnp.int32)
    lane = lax.broadcasted_iota(jnp.int32, (1, 128), 1)
    for k in range(NP):
        starts.append(starts[-1] + lengths[k])
        split = jnp.where((lane == k) | (lane == k + 64), flags[k], split)
    position = (
        dp * (ROWS * 128)
        + lax.broadcasted_iota(jnp.int32, (ROWS, 128), 0) * 128
        + lax.broadcasted_iota(jnp.int32, (ROWS, 128), 1)
    )
    w = state[0]
    w_sums = piece_sums(w * w, position, starts, 0)

    def sum_over_x(zz, high, low, unit):
        landed(x_in.at[pl.ds(0, NX - 1), zz, pl.ds(0, CODED)], xr_sem.at[zz])
        for dx in (1, 3, 2):
            xx = (x + dx) % NX
            h, l = decode(x_in[xx, zz, :WORDS, :], x_in[xx, zz, WORDS:CODED, :], unit)
            high, low = high + h, low + l
        return high, low

    def halves(zz, xx):
        start = pl.multiple_of((zz * NX + xx) * ROWS, ROWS)
        return held[pl.ds(start, WORDS), :], held[pl.ds(pl.multiple_of(start + WORDS, WORDS), WORDS), :]

    def sum_over_near(xx):
        high, low = halves(z, xx)
        for n in range(len(NEAR)):
            h, l = decode(row_in[n, xx, :WORDS, :], row_in[n, xx, WORDS:CODED, :], UNIT_X)
            high, low = high + h, low + l
        return high, low

    pl.semaphore_wait(word_sem, 2)
    for n, o in enumerate(REDUCED):
        if n == OWN_AT:
            load(z).wait()
            landed(row_in.at[:, :, pl.ds(0, CODED)], land_sem.at[3])
            for dx in (2, 1, 3):
                xx = (x + dx) % NX
                words, scale = encode(jnp.concatenate(sum_over_near(xx), axis=0), UNIT_Z)
                coded[xx, z, :WORDS, :] = words
                coded[xx, z, WORDS:CODED, :] = scale
                x_copy(z, dx).start()
            high, low = sum_over_near(x)
            total[:WORDS, :] = high
            total[WORDS:, :] = low
        zz = (z + o) % NZ
        high, low = sum_over_x(zz, *halves(zz, x), UNIT_X)
        if o in MERGED:
            first, count = MERGED[o]
            landed(way_in.at[pl.ds(first, count), pl.ds(0, CODED)], way_sem.at[first])
            for slot in range(first, first + count):
                h, l = decode(way_in[slot, :WORDS, :], way_in[slot, WORDS:CODED, :], UNIT_Z)
                high, low = high + h, low + l
        words, scale = encode(jnp.concatenate([high, low], axis=0), UNIT_Z)
        z_out[n, :WORDS, :] = words
        z_out[n, WORDS:CODED, :] = scale
        if o in BY_WAY:
            to, slot = BY_WAY[o]
            target, sem = way_in.at[slot], way_sem.at[0 if slot < 2 else 2 if slot < 4 else slot]
        else:
            to = o
            target, sem = z_in.at[DIRECT.index(o)], land_sem.at[0]
        pltpu.make_async_remote_copy(
            src_ref=z_out.at[n, pl.ds(0, CODED)], dst_ref=target.at[pl.ds(0, CODED)],
            send_sem=send_sem.at[1], recv_sem=sem,
            device_id=at((z + to) % NZ, x, t), device_id_type=MESH,
        ).start()
    high, low = sum_over_x(z, total[:WORDS, :], total[WORDS:, :], UNIT_Z)
    landed(z_in.at[pl.ds(0, len(DIRECT)), pl.ds(0, CODED)], land_sem.at[0])
    for n in range(len(DIRECT)):
        h, l = decode(z_in[n, :WORDS, :], z_in[n, WORDS:CODED, :], UNIT_Z)
        high, low = high + h, low + l
    total[:WORDS, :] = high
    total[WORDS:, :] = low

    grad = total[...] * (1.0 / (NZ * NX))
    new_avg = 0.9 * state[1] + 0.1 * grad
    new_avg_sq = 0.95 * state[2] + 0.05 * grad * grad
    made[1] = new_avg
    made[2] = new_avg_sq
    update = new_avg / (jnp.sqrt(new_avg_sq) + 1e-08) + 0.1 * state[0]
    total[...] = update
    u_sums = piece_sums(update * update, position, starts, 64)

    mine = z * 2 + core
    stat_z[mine, 0:1, :] = w_sums + u_sums
    line = [(o, dc) for o in FAR_FIRST for dc in (1, 0)] + [(0, 1)]
    for o, dc in line:
        pltpu.make_async_remote_copy(
            src_ref=stat_z.at[mine, pl.ds(0, 1)], dst_ref=stat_z.at[mine, pl.ds(0, 1)],
            send_sem=send_sem.at[2], recv_sem=land_sem.at[1],
            device_id=at((z + o) % NZ, x, y * 2 + (core + dc) % 2), device_id_type=MESH,
        ).start()
    landed(stat_z.at[pl.ds(0, len(line)), pl.ds(0, 1)], land_sem.at[1])
    own = stat_z[core, 0:1, :]
    other = stat_z[1 - core, 0:1, :]
    for zz in range(1, NZ):
        own = own + stat_z[zz * 2 + core, 0:1, :]
        other = other + stat_z[zz * 2 + 1 - core, 0:1, :]
    me = x * NY + y
    stat_p[me, 0:1, :] = own
    stat_p[me, 1:2, :] = own + other
    plane = [(dx, dy) for dx in (2, 1, 3, 0) for dy in (2, 1, 3, 0) if dx or dy]
    for dx, dy in plane:
        pltpu.make_async_remote_copy(
            src_ref=stat_p.at[me, pl.ds(0, 2)], dst_ref=stat_p.at[me, pl.ds(0, 2)],
            send_sem=send_sem.at[3], recv_sem=land_sem.at[2],
            device_id=near(dx, dy, 0), device_id_type=MESH,
        ).start()
    landed(stat_p.at[pl.ds(0, len(plane)), pl.ds(0, 2)], land_sem.at[2])
    data_sum = stat_p[y, 0:1, :]
    for xx in range(1, NX):
        data_sum = data_sum + stat_p[xx * NY + y, 0:1, :]
    tensor_sum = stat_p[0, 1:2, :]
    for i in range(1, NX * NY):
        tensor_sum = tensor_sum + stat_p[i, 1:2, :]
    effective = jnp.where(split == 1, tensor_sum, data_sum)
    norms = jnp.sqrt(effective)
    trust = norms / jnp.maximum(pltpu.roll(norms, 64, 1), 1.0)
    trust_at = jnp.broadcast_to(trust[:, 0:1], (ROWS, 128))
    for k in range(1, NP):
        trust_at = jnp.where(position >= starts[k], trust[:, k : k + 1], trust_at)
    new_weights = state[0] - 0.05 * trust_at * total[...]

    weights[z, x] = new_weights.astype(jnp.bfloat16)

    def g_copy(back, o):
        block = weights.at[(z - back) % NZ, x]
        return pltpu.make_async_remote_copy(
            src_ref=block, dst_ref=block,
            send_sem=send_sem.at[4], recv_sem=load_sem.at[(back + o) % NZ],
            device_id=at((z + o) % NZ, x, t), device_id_type=MESH,
        )

    def f_copy(back, dx):
        block = weights.at[(z - back) % NZ, x]
        return pltpu.make_async_remote_copy(
            src_ref=block, dst_ref=block,
            send_sem=send_sem.at[5], recv_sem=xr_sem.at[back],
            device_id=at(z, (x + dx) % NX, t), device_id_type=MESH,
        )

    def r_copy(o):
        return pltpu.make_async_remote_copy(
            src_ref=weights.at[z], dst_ref=weights.at[z],
            send_sem=send_sem.at[6], recv_sem=way_sem.at[NEAR.index(o)],
            device_id=at((z + o) % NZ, x, t), device_id_type=MESH,
        )

    def spread(back):
        for dx in (2, 1, 3):
            f_copy(back, dx).start()

    for o in LONG:
        g_copy(0, o).start()
    spread(0)
    made[0] = new_weights

    gone(coded.at[pl.ds(0, NX - 1), pl.ds(0, len(REDUCED) + 1), pl.ds(0, CODED)], send_sem.at[0])
    gone(coded.at[:, pl.ds(0, len(NEAR)), pl.ds(0, CODED)], send_sem.at[7])
    gone(z_out.at[pl.ds(0, len(REDUCED)), pl.ds(0, CODED)], send_sem.at[1])
    gone(stat_z.at[pl.ds(0, len(line)), pl.ds(0, 1)], send_sem.at[2])
    gone(stat_p.at[pl.ds(0, len(plane)), pl.ds(0, 2)], send_sem.at[3])

    for back in ARRIVALS:
        landed(weights.at[(z - back) % NZ, x], load_sem.at[back])
        for o in RELAYS.get(back, ()):
            g_copy(back, o).start()
        spread(back)
        if back == 11:
            landed(weights.at[z, pl.ds(0, NX - 1)], xr_sem.at[0])
            for o in NEAR:
                r_copy(o).start()

    for back in (0, 3, 13, 5, 11, 1, 15, 4, 12, 2, 14, 8, 6, 10, 7, 9):
        zz = (z - back) % NZ
        if back in NEAR:
            landed(weights.at[zz], way_sem.at[NEAR.index(back)])
        elif back:
            landed(weights.at[zz, pl.ds(0, NX - 1)], xr_sem.at[back])

        def place(xx, c, zz=zz):
            start = pl.multiple_of((zz * NX + xx) * ROWS, ROWS)
            model[pl.ds(start, ROWS), :, :] = weights[zz, xx][:, None, :]
            return c

        lax.fori_loop(0, NX, place, 0)

    gone(weights.at[pl.ds(0, len(ARRIVALS)), 0], send_sem.at[4])
    gone(weights.at[pl.ds(0, 1 + len(ARRIVALS)), pl.ds(0, NX - 1)], send_sem.at[5])
    gone(weights.at[pl.ds(0, len(NEAR))], send_sem.at[6])


def local(grads, piece_lengths, split_flags, master_params, exp_avg, exp_avg_sq):
    vmem = pl.BlockSpec(memory_space=pltpu.VMEM)
    anywhere = pl.BlockSpec(memory_space=pltpu.HBM)
    dma = pltpu.SemaphoreType.DMA
    hbm = lambda array: pltpu.with_memory_space_constraint(array, pltpu.HBM)
    made, model = pl.pallas_call(
        kernel,
        name="lamb",
        out_shape=(jax.ShapeDtypeStruct((3, ROWS, 128), jnp.float32), jax.ShapeDtypeStruct((NZ * NX * ROWS, 1, 128), jnp.bfloat16)),
        in_specs=[anywhere] * 6,
        out_specs=(vmem, vmem),
        scratch_shapes=[
            pltpu.VMEM((NZ, NX, ROWS, 128), jnp.bfloat16),
            pltpu.VMEM((NZ * NX * ROWS, 128), jnp.float32),
            pltpu.VMEM((NX, NZ, WORDS + 8, 128), jnp.int32),
            pltpu.VMEM((len(NEAR), NX, WORDS + 8, 128), jnp.int32),
            pltpu.VMEM((NX, NZ, WORDS + 8, 128), jnp.int32),
            pltpu.VMEM((NZ, WORDS + 8, 128), jnp.int32),
            pltpu.VMEM((len(BY_WAY), WORDS + 8, 128), jnp.int32),
            pltpu.VMEM((len(DIRECT), WORDS + 8, 128), jnp.int32),
            pltpu.VMEM((ROWS, 128), jnp.float32),
            pltpu.VMEM((3, ROWS, 128), jnp.float32),
            pltpu.VMEM((NZ * 2, 8, 128), jnp.float32),
            pltpu.VMEM((NX * NY, 8, 128), jnp.float32),
            pltpu.SMEM((NP,), jnp.int32),
            pltpu.SMEM((NP,), jnp.int32),
            pltpu.SemaphoreType.REGULAR, dma((NZ,)), dma((3,)), dma((8,)), dma((4,)), dma((NZ,)), dma((6,)),
        ],
        compiler_params=pltpu.CompilerParams(
            collective_id=0, has_side_effects=True, vmem_limit_bytes=24 * 2**20
        ),
    )(
        hbm(piece_lengths), hbm(split_flags), hbm(grads.reshape(NZ * NX * ROWS, 128)),
        hbm(master_params.reshape(ROWS, 128)), hbm(exp_avg.reshape(ROWS, 128)), hbm(exp_avg_sq.reshape(ROWS, 128)),
    )
    return (
        made[0].reshape(1, -1), made[1].reshape(1, -1), made[2].reshape(1, -1), model.reshape(1, -1)
    )


def solution(mesh):
    return jax.shard_map(
        local,
        mesh=mesh,
        in_specs=(
            P("dp", "tensor", None),
            P(),
            P(),
            P("tensor", "dp"),
            P("tensor", "dp"),
            P("tensor", "dp"),
        ),
        out_specs=(P("tensor", "dp"), P("tensor", "dp"), P("tensor", "dp"), P("tensor", None)),
        check_vma=False,
    )
```

```python
import jax
import jax.numpy as jnp
from jax import lax
from jax.experimental import pallas as pl
from jax.experimental.pallas import tpu as pltpu
from jax.sharding import PartitionSpec as P

MESH = pl.DeviceIdType.MESH
NZ, NX, NY, NT = 16, 4, 4, 8
ROWS = 64
WORDS = 32
NP = 40
CODED = WORDS + 1


def encode(block, unit):
    top = jnp.max(jnp.abs(block), axis=0, keepdims=True)
    scale = (top * unit).astype(jnp.int32) + 1
    inverse = (32767.0 * unit) / scale.astype(jnp.float32)
    codes = jnp.round(block * inverse).astype(jnp.int32)
    return (codes[:WORDS] << 16) + codes[WORDS:], scale


def decode(words, scale, unit):
    step = scale.astype(jnp.float32) * (1.0 / (32767.0 * unit))
    high = ((words + 32768) >> 16).astype(jnp.float32) * step
    low = ((words << 16) >> 16).astype(jnp.float32) * step
    return high, low


NEAR = (2, 14, 1, 15)
LONG = (8, 5, 11, 3, 13)
RELAYS = {3: (1,), 13: (15,), 5: (2, 1), 11: (14, 15), 8: ()}
ARRIVALS = (3, 13, 5, 11, 4, 12, 8, 6, 10, 7, 9)
REDUCED = (8, 7, 9, 6, 10, 4, 12, 5, 11, 3, 13)
SENT = (8, 2, 14, 7, 1, 15, 9, 6, 10, 4, 12, 5, 11, 3, 13)
BY_WAY = {7: (2, 0), 6: (1, 1), 9: (14, 2), 10: (15, 3), 4: (1, 4), 12: (15, 5)}
MERGED = {5: (0, 2), 11: (2, 2), 3: (4, 1), 13: (5, 1)}
OWN_AT = 8
DIRECT = (8, 5, 11, 3, 13)
FAR_FIRST = (8, 7, 9, 6, 10, 5, 11, 4, 12, 3, 13, 2, 14, 1, 15)

UNIT_X = float(2**26)
UNIT_Z = float(2**23)


def piece_sums(values, position, starts, first):
    rows = []
    for k in range(NP):
        inside = (position >= starts[k]) & (position < starts[k + 1])
        rows.append(jnp.sum(jnp.where(inside, values, 0.0), axis=0, keepdims=True))
    table = jnp.concatenate(rows, axis=0)
    totals = jnp.sum(table, axis=1, keepdims=True)
    piece = lax.broadcasted_iota(jnp.int32, (NP, 128), 0)
    lane = lax.broadcasted_iota(jnp.int32, (NP, 128), 1)
    return jnp.sum(jnp.where(piece + first == lane, totals, 0.0), axis=0, keepdims=True)


def kernel(
    lengths_in, flags_in, grads, master, avg, avg_sq,
    made, model,
    weights, held, coded, row_in, x_in, z_out, way_in, z_in, total, state, stat_z, stat_p, lengths, flags,
    word_sem, load_sem, state_sem, send_sem, land_sem, xr_sem, way_sem,
):
    dp = lax.axis_index("dp")
    t = lax.axis_index("tensor")
    z, x = dp // NX, dp % NX

    def at(zz, xx, tt):
        return (zz * NX + xx, tt)

    def landed(ref, sem):
        pltpu.make_async_remote_copy(
            src_ref=ref, dst_ref=ref, send_sem=sem, recv_sem=sem,
            device_id=at(z, (x + 1) % NX, t), device_id_type=MESH,
        ).wait_recv()

    def gone(ref, sem):
        pltpu.make_async_remote_copy(
            src_ref=ref, dst_ref=ref, send_sem=sem, recv_sem=sem,
            device_id=at(z, (x + 1) % NX, t), device_id_type=MESH,
        ).wait_send()

    barrier = pltpu.get_barrier_semaphore()

    y, core = t // 2, t % 2

    def near(dx, dy, dc):
        return at(z, (x + dx) % NX, ((y + dy) % NY) * 2 + (core + dc) % 2)

    greeted = [at((z + o) % NZ, x, t) for o in (4, 12, 3, 13, 2, 14, 1, 15)]
    greeted += [near(dx, 0, 0) for dx in range(1, NX)]
    greeted += [near(0, dy, dc) for dy in range(NY) for dc in range(2) if dy or dc]
    for device in greeted:
        pl.semaphore_signal(barrier, 1, device_id=device, device_id_type=MESH)

    def load(zz):
        rows = pl.ds(pl.multiple_of(zz * (NX * ROWS), NX * ROWS), NX * ROWS)
        return pltpu.make_async_copy(grads.at[rows], held.at[rows], load_sem.at[zz])

    for o in (*SENT, 0):
        load((z + o) % NZ).start()

    def x_copy(zz, dx):
        xx = (x + dx) % NX
        return pltpu.make_async_remote_copy(
            src_ref=coded.at[xx, zz, pl.ds(0, CODED)], dst_ref=x_in.at[x, zz, pl.ds(0, CODED)],
            send_sem=send_sem.at[0], recv_sem=xr_sem.at[zz],
            device_id=at(z, xx, t), device_id_type=MESH,
        )

    pl.semaphore_wait(barrier, len(greeted))
    for o in (4, 12):
        pl.semaphore_signal(word_sem, 1, device_id=at((z + o) % NZ, x, t), device_id_type=MESH)

    def code(zz, xx):
        start = pl.multiple_of((zz * NX + xx) * ROWS, ROWS)
        words, scale = encode(held[pl.ds(start, ROWS), :], UNIT_X)
        coded[xx, zz, :WORDS, :] = words
        coded[xx, zz, WORDS:CODED, :] = scale

    tables = [
        pltpu.make_async_copy(lengths_in, lengths, state_sem.at[1]),
        pltpu.make_async_copy(flags_in, flags, state_sem.at[2]),
    ]
    for n, o in enumerate(SENT):
        if n == 3:
            for i, ref in enumerate((master, avg, avg_sq)):
                pltpu.make_async_copy(ref, state.at[i], state_sem.at[0]).start()
            for copy in tables:
                copy.start()
        zz = (z + o) % NZ
        load(zz).wait()
        if o in NEAR:
            for xx in range(NX):
                code(zz, xx)
            pltpu.make_async_remote_copy(
                src_ref=coded.at[:, zz, pl.ds(0, CODED)],
                dst_ref=row_in.at[NEAR.index(o), :, pl.ds(0, CODED)],
                send_sem=send_sem.at[7], recv_sem=land_sem.at[3],
                device_id=at(zz, x, t), device_id_type=MESH,
            ).start()
        else:
            for dx in (2, 1, 3):
                code(zz, (x + dx) % NX)
                x_copy(zz, dx).start()

    for copy in tables:
        copy.wait()
    pltpu.make_async_copy(state, state, state_sem.at[0]).wait()
    starts = [jnp.int32(0)]
    split = jnp.zeros((1, 128), jnp.int32)
    lane = lax.broadcasted_iota(jnp.int32, (1, 128), 1)
    for k in range(NP):
        starts.append(starts[-1] + lengths[k])
        split = jnp.where((lane == k) | (lane == k + 64), flags[k], split)
    position = (
        dp * (ROWS * 128)
        + lax.broadcasted_iota(jnp.int32, (ROWS, 128), 0) * 128
        + lax.broadcasted_iota(jnp.int32, (ROWS, 128), 1)
    )
    w = state[0]
    w_sums = piece_sums(w * w, position, starts, 0)

    def sum_over_x(zz, high, low, unit):
        landed(x_in.at[pl.ds(0, NX - 1), zz, pl.ds(0, CODED)], xr_sem.at[zz])
        for dx in (1, 3, 2):
            xx = (x + dx) % NX
            h, l = decode(x_in[xx, zz, :WORDS, :], x_in[xx, zz, WORDS:CODED, :], unit)
            high, low = high + h, low + l
        return high, low

    def halves(zz, xx):
        start = pl.multiple_of((zz * NX + xx) * ROWS, ROWS)
        return held[pl.ds(start, WORDS), :], held[pl.ds(pl.multiple_of(start + WORDS, WORDS), WORDS), :]

    def sum_over_near(xx):
        high, low = halves(z, xx)
        for n in range(len(NEAR)):
            h, l = decode(row_in[n, xx, :WORDS, :], row_in[n, xx, WORDS:CODED, :], UNIT_X)
            high, low = high + h, low + l
        return high, low

    pl.semaphore_wait(word_sem, 2)
    for n, o in enumerate(REDUCED):
        if n == OWN_AT:
            load(z).wait()
            landed(row_in.at[:, :, pl.ds(0, CODED)], land_sem.at[3])
            for dx in (2, 1, 3):
                xx = (x + dx) % NX
                words, scale = encode(jnp.concatenate(sum_over_near(xx), axis=0), UNIT_Z)
                coded[xx, z, :WORDS, :] = words
                coded[xx, z, WORDS:CODED, :] = scale
                x_copy(z, dx).start()
            high, low = sum_over_near(x)
            total[:WORDS, :] = high
            total[WORDS:, :] = low
        zz = (z + o) % NZ
        high, low = sum_over_x(zz, *halves(zz, x), UNIT_X)
        if o in MERGED:
            first, count = MERGED[o]
            landed(way_in.at[pl.ds(first, count), pl.ds(0, CODED)], way_sem.at[first])
            for slot in range(first, first + count):
                h, l = decode(way_in[slot, :WORDS, :], way_in[slot, WORDS:CODED, :], UNIT_Z)
                high, low = high + h, low + l
        words, scale = encode(jnp.concatenate([high, low], axis=0), UNIT_Z)
        z_out[n, :WORDS, :] = words
        z_out[n, WORDS:CODED, :] = scale
        if o in BY_WAY:
            to, slot = BY_WAY[o]
            target, sem = way_in.at[slot], way_sem.at[0 if slot < 2 else 2 if slot < 4 else slot]
        else:
            to = o
            target, sem = z_in.at[DIRECT.index(o)], land_sem.at[0]
        pltpu.make_async_remote_copy(
            src_ref=z_out.at[n, pl.ds(0, CODED)], dst_ref=target.at[pl.ds(0, CODED)],
            send_sem=send_sem.at[1], recv_sem=sem,
            device_id=at((z + to) % NZ, x, t), device_id_type=MESH,
        ).start()
    high, low = sum_over_x(z, total[:WORDS, :], total[WORDS:, :], UNIT_Z)
    landed(z_in.at[pl.ds(0, len(DIRECT)), pl.ds(0, CODED)], land_sem.at[0])
    for n in range(len(DIRECT)):
        h, l = decode(z_in[n, :WORDS, :], z_in[n, WORDS:CODED, :], UNIT_Z)
        high, low = high + h, low + l
    total[:WORDS, :] = high
    total[WORDS:, :] = low

    grad = total[...] * (1.0 / (NZ * NX))
    new_avg = 0.9 * state[1] + 0.1 * grad
    new_avg_sq = 0.95 * state[2] + 0.05 * grad * grad
    made[1] = new_avg
    made[2] = new_avg_sq
    update = new_avg / (jnp.sqrt(new_avg_sq) + 1e-08) + 0.1 * state[0]
    total[...] = update
    u_sums = piece_sums(update * update, position, starts, 64)

    mine = z * 2 + core
    stat_z[mine, 0:1, :] = w_sums + u_sums
    line = [(o, dc) for o in FAR_FIRST for dc in (1, 0)] + [(0, 1)]
    for o, dc in line:
        pltpu.make_async_remote_copy(
            src_ref=stat_z.at[mine, pl.ds(0, 1)], dst_ref=stat_z.at[mine, pl.ds(0, 1)],
            send_sem=send_sem.at[2], recv_sem=land_sem.at[1],
            device_id=at((z + o) % NZ, x, y * 2 + (core + dc) % 2), device_id_type=MESH,
        ).start()
    landed(stat_z.at[pl.ds(0, len(line)), pl.ds(0, 1)], land_sem.at[1])
    own = stat_z[core, 0:1, :]
    other = stat_z[1 - core, 0:1, :]
    for zz in range(1, NZ):
        own = own + stat_z[zz * 2 + core, 0:1, :]
        other = other + stat_z[zz * 2 + 1 - core, 0:1, :]
    me = x * NY + y
    stat_p[me, 0:1, :] = own
    stat_p[me, 1:2, :] = own + other
    plane = [(dx, dy) for dx in (2, 1, 3, 0) for dy in (2, 1, 3, 0) if dx or dy]
    for dx, dy in plane:
        pltpu.make_async_remote_copy(
            src_ref=stat_p.at[me, pl.ds(0, 2)], dst_ref=stat_p.at[me, pl.ds(0, 2)],
            send_sem=send_sem.at[3], recv_sem=land_sem.at[2],
            device_id=near(dx, dy, 0), device_id_type=MESH,
        ).start()
    landed(stat_p.at[pl.ds(0, len(plane)), pl.ds(0, 2)], land_sem.at[2])
    data_sum = stat_p[y, 0:1, :]
    for xx in range(1, NX):
        data_sum = data_sum + stat_p[xx * NY + y, 0:1, :]
    tensor_sum = stat_p[0, 1:2, :]
    for i in range(1, NX * NY):
        tensor_sum = tensor_sum + stat_p[i, 1:2, :]
    effective = jnp.where(split == 1, tensor_sum, data_sum)
    norms = jnp.sqrt(effective)
    trust = norms / jnp.maximum(pltpu.roll(norms, 64, 1), 1.0)
    trust_at = jnp.broadcast_to(trust[:, 0:1], (ROWS, 128))
    for k in range(1, NP):
        trust_at = jnp.where(position >= starts[k], trust[:, k : k + 1], trust_at)
    new_weights = state[0] - 0.05 * trust_at * total[...]

    weights[z, x] = new_weights.astype(jnp.bfloat16)

    def g_copy(back, o):
        block = weights.at[(z - back) % NZ, x]
        return pltpu.make_async_remote_copy(
            src_ref=block, dst_ref=block,
            send_sem=send_sem.at[4], recv_sem=load_sem.at[(back + o) % NZ],
            device_id=at((z + o) % NZ, x, t), device_id_type=MESH,
        )

    def f_copy(back, dx):
        block = weights.at[(z - back) % NZ, x]
        return pltpu.make_async_remote_copy(
            src_ref=block, dst_ref=block,
            send_sem=send_sem.at[5], recv_sem=xr_sem.at[back],
            device_id=at(z, (x + dx) % NX, t), device_id_type=MESH,
        )

    def r_copy(o):
        return pltpu.make_async_remote_copy(
            src_ref=weights.at[z], dst_ref=weights.at[z],
            send_sem=send_sem.at[6], recv_sem=way_sem.at[NEAR.index(o)],
            device_id=at((z + o) % NZ, x, t), device_id_type=MESH,
        )

    def spread(back):
        for dx in (2, 1, 3):
            f_copy(back, dx).start()

    for o in LONG:
        g_copy(0, o).start()
    spread(0)
    made[0] = new_weights

    gone(coded.at[pl.ds(0, NX - 1), pl.ds(0, len(REDUCED) + 1), pl.ds(0, CODED)], send_sem.at[0])
    gone(coded.at[:, pl.ds(0, len(NEAR)), pl.ds(0, CODED)], send_sem.at[7])
    gone(z_out.at[pl.ds(0, len(REDUCED)), pl.ds(0, CODED)], send_sem.at[1])
    gone(stat_z.at[pl.ds(0, len(line)), pl.ds(0, 1)], send_sem.at[2])
    gone(stat_p.at[pl.ds(0, len(plane)), pl.ds(0, 2)], send_sem.at[3])

    for back in ARRIVALS:
        landed(weights.at[(z - back) % NZ, x], load_sem.at[back])
        for o in RELAYS.get(back, ()):
            g_copy(back, o).start()
        spread(back)
        if back == 11:
            landed(weights.at[z, pl.ds(0, NX - 1)], xr_sem.at[0])
            for o in NEAR:
                r_copy(o).start()

    for back in (0, 3, 13, 5, 11, 1, 15, 4, 12, 2, 14, 8, 6, 10, 7, 9):
        zz = (z - back) % NZ
        if back in NEAR:
            landed(weights.at[zz], way_sem.at[NEAR.index(back)])
        elif back:
            landed(weights.at[zz, pl.ds(0, NX - 1)], xr_sem.at[back])

        def place(xx, c, zz=zz):
            start = pl.multiple_of((zz * NX + xx) * ROWS, ROWS)
            model[pl.ds(start, ROWS), :, :] = weights[zz, xx][:, None, :]
            return c

        lax.fori_loop(0, NX, place, 0)

    gone(weights.at[pl.ds(0, len(ARRIVALS)), 0], send_sem.at[4])
    gone(weights.at[pl.ds(0, 1 + len(ARRIVALS)), pl.ds(0, NX - 1)], send_sem.at[5])
    gone(weights.at[pl.ds(0, len(NEAR))], send_sem.at[6])


def local(grads, piece_lengths, split_flags, master_params, exp_avg, exp_avg_sq):
    vmem = pl.BlockSpec(memory_space=pltpu.VMEM)
    anywhere = pl.BlockSpec(memory_space=pltpu.HBM)
    dma = pltpu.SemaphoreType.DMA
    hbm = lambda array: pltpu.with_memory_space_constraint(array, pltpu.HBM)
    made, model = pl.pallas_call(
        kernel,
        name="lamb",
        out_shape=(jax.ShapeDtypeStruct((3, ROWS, 128), jnp.float32), jax.ShapeDtypeStruct((NZ * NX * ROWS, 1, 128), jnp.bfloat16)),
        in_specs=[anywhere] * 6,
        out_specs=(vmem, vmem),
        scratch_shapes=[
            pltpu.VMEM((NZ, NX, ROWS, 128), jnp.bfloat16),
            pltpu.VMEM((NZ * NX * ROWS, 128), jnp.float32),
            pltpu.VMEM((NX, NZ, WORDS + 8, 128), jnp.int32),
            pltpu.VMEM((len(NEAR), NX, WORDS + 8, 128), jnp.int32),
            pltpu.VMEM((NX, NZ, WORDS + 8, 128), jnp.int32),
            pltpu.VMEM((NZ, WORDS + 8, 128), jnp.int32),
            pltpu.VMEM((len(BY_WAY), WORDS + 8, 128), jnp.int32),
            pltpu.VMEM((len(DIRECT), WORDS + 8, 128), jnp.int32),
            pltpu.VMEM((ROWS, 128), jnp.float32),
            pltpu.VMEM((3, ROWS, 128), jnp.float32),
            pltpu.VMEM((NZ * 2, 8, 128), jnp.float32),
            pltpu.VMEM((NX * NY, 8, 128), jnp.float32),
            pltpu.SMEM((NP,), jnp.int32),
            pltpu.SMEM((NP,), jnp.int32),
            pltpu.SemaphoreType.REGULAR, dma((NZ,)), dma((3,)), dma((8,)), dma((4,)), dma((NZ,)), dma((6,)),
        ],
        compiler_params=pltpu.CompilerParams(
            collective_id=0, has_side_effects=True, vmem_limit_bytes=24 * 2**20
        ),
    )(
        hbm(piece_lengths), hbm(split_flags), hbm(grads.reshape(NZ * NX * ROWS, 128)),
        hbm(master_params.reshape(ROWS, 128)), hbm(exp_avg.reshape(ROWS, 128)), hbm(exp_avg_sq.reshape(ROWS, 128)),
    )
    return (
        made[0].reshape(1, -1), made[1].reshape(1, -1), made[2].reshape(1, -1), model.reshape(1, -1)
    )


def solution(mesh):
    return jax.shard_map(
        local,
        mesh=mesh,
        in_specs=(
            P("dp", "tensor", None),
            P(),
            P(),
            P("tensor", "dp"),
            P("tensor", "dp"),
            P("tensor", "dp"),
        ),
        out_specs=(P("tensor", "dp"), P("tensor", "dp"), P("tensor", "dp"), P("tensor", None)),
        check_vma=False,
    )
```
